256 devices in a mesh: img: 16 (over x_lo, z), vol: 16 (over x_hi, y, core).
Axes of the slice: x: 4 (x_hi: 2, x_lo: 2; x = x_hi * 2 + x_lo), y: 4, z: 8, core: 2. Of those that a mesh axis runs over, the one named last changes fastest.
Arguments:
- orientations: int32 [512, 4], P('img'), may hold values from 0 to 255
- images: bfloat16 [512, 16, 1280], P(('img', 'vol')), may hold values from -6 to 6
- ctf_values: bfloat16 [512, 16, 640], P(('img', 'vol')), may hold values from -1 to 1
- volume: bfloat16 [8192, 1280], P('vol'), may hold values from -6 to 6
- line_index: int32 [256, 16], replicated, may hold values from 0 to 8191
- line_weight: float32 [256, 16], replicated, may hold values from 0.1 to 0.9
- noise_ratio: float32 [8192], P(('vol', 'img')), may hold values from 0.3 to 3
Outputs:
- assignment: float32 [512, 4], P(('img', 'vol'))
- density_map: float32 [8192, 1280], P(('vol', 'img'))
The draws below stay inside these ranges and needn't reach their ends.
All inputs are finite; a program needn't handle non-finite values.
Results may differ from the reference program's by a relative error of at most 0.018.
Values may be sent and summed in bfloat16 or wider, within the bound.
No kernel may reach another device: no remote copies, remote signals or barrier semaphores. Data moves between devices by JAX's collectives and lax.ppermute only.
A program may use at most 128 MiB of HBM per device.

```python
import math
import jax
import jax.numpy as jnp
import numpy as np
from jax import lax

K = 640
S = 16
NORIENT = 256
SLOTS = 4
IMAGES = 512
LINES = 8192


def set_ends(entries, key, least, largest):
    extent = entries.shape
    place = [jax.random.randint(jax.random.fold_in(key, axis), (), 0, extent[axis]) for axis in range(len(extent))]
    entries = entries.at[tuple(place)].set(least)
    longest = extent.index(max(extent))
    place[longest] = (place[longest] + 1) % extent[longest]
    return entries.at[tuple(place)].set(largest)


def block_scale(stream_key, extent, pieces, least, top_value):
    gain, own = 1.0, jax.random.fold_in(stream_key, 6)
    for position, blocks in pieces:
        steps = jnp.exp(jax.random.uniform(jax.random.fold_in(own, position), (blocks,), jnp.float32, least / len(pieces), top_value / len(pieces)))
        gain = gain * jnp.repeat(steps, extent[position] // blocks).reshape([-1 if axis == position else 1 for axis in range(len(extent))])
    return gain


def cumulative_ranks(count, skew):
    weights = [(1 << 20) // math.isqrt(grade ** skew) + 1 for grade in range(1, count + 1)]
    scale = 1 + sum(weights) // (1 << 30)
    return np.cumsum(np.array([max(1, weight // scale) for weight in weights]))


def skewed_ids(stream_key, shape, amount, slope):
    listing = cumulative_ranks(amount, slope)
    lot = jax.random.randint(jax.random.fold_in(stream_key, 1), shape, 0, int(listing[amount - 1]))
    standing = jnp.searchsorted(jnp.asarray(listing, jnp.int32), lot, side="right")
    return jax.random.permutation(jax.random.fold_in(stream_key, 2), amount)[standing].astype(jnp.int32)


def noise(rng, extent, width, limit, pieces=(), kind=jnp.bfloat16):
    entries = width * jax.random.normal(rng, extent, jnp.float32)
    if pieces:
        entries = entries * block_scale(rng, extent, pieces, -0.22, 0.18)
    return jnp.clip(entries, -limit, limit).astype(kind)


def setup_inputs(seed: int = 0) -> dict:
    streams_of = jax.random.split(jax.random.key(seed), 8)
    orientations = set_ends(skewed_ids(streams_of[0], (IMAGES, SLOTS), NORIENT, 2), jax.random.fold_in(streams_of[0], 3), 0, NORIENT - 1).astype(jnp.int32)
    images = noise(streams_of[1], (IMAGES, S, 2 * K), 1.0, 6.0, ((0, 256),))
    ctf_values = jnp.clip(jax.random.uniform(streams_of[2], (IMAGES, S, K), jnp.float32, -1.0, 1.0) * block_scale(streams_of[2], (IMAGES, S, K), ((0, 256),), -0.4, 0.0), -1.0, 1.0).astype(jnp.bfloat16)
    volume = noise(streams_of[3], (LINES, 2 * K), 1.0, 6.0, ((0, 16),))
    line_index = set_ends(jax.random.randint(streams_of[4], (NORIENT, S), 0, LINES), jax.random.fold_in(streams_of[4], 1), 0, LINES - 1).astype(jnp.int32)
    line_weight = jnp.clip(jax.random.uniform(streams_of[5], (NORIENT, S), jnp.float32, 0.1, 0.9), 0.1, 0.9)
    noise_ratio = jnp.clip(jnp.exp(math.log(3.0) - 2.3025851 * jax.random.uniform(streams_of[6], (LINES,), jnp.float32) ** block_scale(streams_of[6], (LINES,), ((0, 256),), -0.2, 0.2)), 0.3, 3.0)
    return {"orientations": orientations, "images": images, "ctf_values": ctf_values, "volume": volume, "line_index": line_index, "line_weight": line_weight, "noise_ratio": noise_ratio}


def reference(orientations, images, ctf_values, volume, line_index, line_weight, noise_ratio):
    lower_line = line_index[orientations].astype(jnp.int32)
    upper_line = ((lower_line + 1) % LINES).astype(jnp.int32)
    picked = line_weight[orientations]
    lower_tap = lax.optimization_barrier(picked.astype(jnp.bfloat16)).astype(jnp.float32)
    upper_tap = lax.optimization_barrier((1.0 - picked).astype(jnp.bfloat16)).astype(jnp.float32)
    norm_scale = 1.0 / math.sqrt(2.0 * S * K)

    def one_image(accum, packed):
        picture, transfer, lower, upper, lower_w, upper_w = packed
        slices = lower_w[..., None] * volume[lower].astype(jnp.float32) + upper_w[..., None] * volume[upper].astype(jnp.float32)
        transfer = transfer.astype(jnp.float32)
        doubled = jnp.concatenate([transfer, transfer], axis=-1)
        weighted = doubled * picture.astype(jnp.float32)
        scores = lax.optimization_barrier(jnp.sum(weighted[None] * slices, axis=(1, 2))) * norm_scale
        raised = jnp.exp(3.0 * jnp.tanh(scores))
        probability = raised / jnp.sum(raised)
        contrib = jnp.concatenate([probability[:, None, None] * weighted[None], probability[:, None, None] * (transfer * transfer)[None]], axis=-1)
        rows = lax.optimization_barrier(contrib.astype(jnp.bfloat16)).astype(jnp.float32).reshape(-1, 3 * K)
        accum = accum.at[lower.reshape(-1)].add(lower_w.reshape(-1, 1) * rows)
        accum = accum.at[upper.reshape(-1)].add(upper_w.reshape(-1, 1) * rows)
        return (accum, probability)
    start_accum = jnp.zeros((LINES, 3 * K), jnp.float32)
    accum, assignment = lax.scan(one_image, start_accum, (images, ctf_values, lower_line, upper_line, lower_tap, upper_tap))
    denom = accum[:, 2 * K:] + noise_ratio[:, None]
    spectrum = (accum[:, :K] + 1j * accum[:, K:2 * K]) / denom
    field = jnp.fft.ifft(spectrum, axis=-1) * math.sqrt(K)
    density_map = jnp.concatenate([jnp.real(field), jnp.imag(field)], axis=-1).astype(jnp.float32)
    return (assignment, density_map)
```

```python
import functools
import math

import jax
import jax.numpy as jnp
import numpy as np
from jax import lax
from jax.experimental import pallas as pl
from jax.experimental.pallas import tpu as pltpu
from jax.sharding import PartitionSpec as P

WIDTH = 640
ROWS = 16
TABLE = 256
SLOTS = 4
LINES = 8192
BANDS = ((0, 1, 4), (2, 3, 4))
LANE = 128
BLOCK = 32
DEVICES = 256
FACTOR = (5, 5, 6, 6, 7, 5, 6, 7)
ORDER = ("vol", "img")
VMEM_LIMIT = 48 * 1024 * 1024

f32 = jnp.float32
bf16 = jnp.bfloat16


def columns_of(half):
    first, second, last = BANDS[half]
    re = lambda band: LANE * band
    im = lambda band: WIDTH + LANE * band
    return (re(first), im(first), re(second), im(second), im(last) if half else re(last))


def inverse_rows():
    k = np.arange(WIDTH)
    angle = (np.outer(k, k) % WIDTH) * (2.0 * np.pi / WIDTH)
    cosine, sine = np.cos(angle), np.sin(angle)
    table = np.concatenate(
        [np.concatenate([cosine, sine], 1), np.concatenate([-sine, cosine], 1)], 0
    ) / np.sqrt(WIDTH)
    starts = [columns_of(0), columns_of(1)]
    rows = [
        np.arange(starts[half][c], starts[half][c] + LANE) for c in range(5) for half in range(2)
    ]
    return np.asarray(table[np.concatenate(rows)], dtype=jnp.bfloat16)


def iota(shape, dim):
    return lax.broadcasted_iota(jnp.int32, shape, dim)


def dot(a, b, dims, precision=None):
    return lax.dot_general(a, b, (dims, ((), ())), precision=precision, preferred_element_type=f32)


def pack_kernel(
    place, images_in, ctf_in, volume_in, orientations_in, noise_in, out,
    images, ctf, volume, orientations, noise, wide, done,
):
    copies = [
        pltpu.make_async_copy(source, target, done.at[n])
        for n, (source, target) in enumerate(
            (
                (orientations_in, orientations),
                (noise_in, noise),
                (images_in, images),
                (ctf_in, ctf),
                (volume_in.at[pl.ds(pl.multiple_of(place[0] * BLOCK, BLOCK), BLOCK), :], volume),
            )
        )
    ]
    for copy in copies:
        copy.start()
    source, target = iota((256, 256), 0), iota((256, 256), 1)
    moved = (source // 16 % 2) * 128 + (source % 16) * 8 + source // 32
    shuffle = jnp.where(target == moved, 1.0, 0.0).astype(bf16)
    same = jnp.where(target == source, 1.0, 0.0).astype(bf16)
    for copy in copies:
        copy.wait()
    own = place[1] * 2
    row8 = iota((16, LANE), 0)
    asked = jnp.zeros((16, LANE), f32)
    for r in range(2 * SLOTS):
        value = orientations[r % SLOTS, own + r // SLOTS].astype(f32)
        asked = jnp.where(row8 == r, value, asked)
    row32 = iota((BLOCK, LANE), 0)
    ratio = jnp.zeros((BLOCK, LANE), f32)
    for r in range(BLOCK):
        ratio = jnp.where(row32 == r, noise[r], ratio)
    ratio_top = ratio.astype(bf16)
    ratio_rest = (ratio - ratio_top.astype(f32)).astype(bf16)
    common = [asked.astype(bf16), ratio_top, ratio_rest, jnp.zeros((16, LANE), bf16)]
    for half in range(2):
        starts = columns_of(half)
        pieces = [images[:, start : start + LANE] for start in starts]
        pieces += [ctf[:, LANE * band : LANE * band + LANE] for band in BANDS[half]]
        pictures = jnp.concatenate(pieces, axis=0)
        others = jnp.concatenate([volume[:, start : start + LANE] for start in starts] + common, axis=0)
        left = dot(pictures, shuffle, ((0,), (0,)))
        right = dot(others, same, ((0,), (0,)))
        base = half * 4 * LANE
        wide[pl.ds(base, LANE, stride=4), :] = left[:, :LANE]
        wide[pl.ds(base + 1, LANE, stride=4), :] = left[:, LANE:]
        wide[pl.ds(base + 2, LANE, stride=4), :] = right[:, :LANE]
        wide[pl.ds(base + 3, LANE, stride=4), :] = right[:, LANE:]
    out[...] = wide[...].astype(bf16)


def taps(lower, weight, s):
    line = lower[s : s + 1, :]
    low = weight[s : s + 1, :]
    low_tap = low.astype(bf16).astype(f32)
    high_tap = (1.0 - low).astype(bf16).astype(f32)
    block = lax.shift_right_logical(line, 5)
    place = jnp.bitwise_and(line, BLOCK - 1)
    rows = iota((BLOCK, TABLE), 0)
    nothing = jnp.zeros((BLOCK, TABLE), f32)
    inside = jnp.where(rows == place, low_tap, jnp.where(rows == place + 1, high_tap, nothing))
    beyond = jnp.where(place == BLOCK - 1, high_tap, 0.0)
    chosen = jnp.where(iota((DEVICES, TABLE), 0) == block, 1.0, 0.0).astype(bf16)
    return chosen, inside, beyond


def score_kernel(got, line_index, line_weight, part, weighted, misc, lower, weight, wide, done):
    copies = [
        pltpu.make_async_copy(line_index, lower, done.at[0]),
        pltpu.make_async_copy(line_weight, weight, done.at[1]),
    ]
    for copy in copies:
        copy.start()
    wide[...] = got[...].astype(f32)
    quarter = [wide[pl.ds(a, DEVICES, stride=4), :].T for a in range(4)]
    to, frm = iota((LANE, LANE), 0), iota((LANE, LANE), 1)
    spread = jnp.zeros((LANE, LANE), f32)
    for c, factor in enumerate(FACTOR):
        spread = jnp.where((to % 8 == c) & (frm == to - c + factor), 1.0, spread)
    spread = spread.astype(bf16)
    for n in range(2):
        weighted[n * LANE : (n + 1) * LANE, :] = quarter[n] * dot(
            spread, quarter[n].astype(bf16), ((1,), (0,))
        )
    misc[0:8, :] = quarter[3][32:40, :]
    misc[8:40, :] = quarter[3][48:80, :] + quarter[3][80:112, :]
    lines = jnp.concatenate([quarter[2], quarter[3][:BLOCK]], axis=0)
    following = [pltpu.roll(lines[c * BLOCK : c * BLOCK + 8], DEVICES - 1, 1)[0:1] for c in range(5)]
    lines = jnp.concatenate([lines] + following + [jnp.zeros((11, DEVICES), f32)], axis=0).astype(bf16)
    for copy in copies:
        copy.wait()
    tables = []
    for s in range(ROWS):
        chosen, inside, beyond = taps(lower, weight, s)
        found = dot(lines, chosen, ((1,), (0,)))
        for c in range(5):
            tables.append(
                jnp.sum(found[c * BLOCK : (c + 1) * BLOCK] * inside, axis=0, keepdims=True)
                + found[5 * BLOCK + c : 5 * BLOCK + c + 1] * beyond
            )
        tables.append(jnp.zeros((3, TABLE), f32))
    slices = jnp.concatenate(tables, axis=0)
    number = iota((TABLE, DEVICES), 0).astype(f32)
    sums = []
    for n in range(2):
        products = dot(
            slices, weighted[n * LANE : (n + 1) * LANE, :], ((0,), (0,)), lax.Precision.HIGHEST
        )
        for o in range(SLOTS):
            asked = misc[n * SLOTS + o : n * SLOTS + o + 1, :]
            sums.append(jnp.sum(jnp.where(number == asked, products, 0.0), axis=0, keepdims=True))
    part[...] = jnp.broadcast_to(jnp.concatenate(sums, axis=0)[None], part.shape)


def relay_kernel(got, out):
    out[...] = jnp.broadcast_to(jnp.sum(got[...], axis=0, keepdims=True), out.shape)


def back_kernel(place, got, weighted, misc, lower, weight, out, assignment, spreads, blocks, wide, norm_scale):
    scores = jnp.sum(got[...], axis=0) * norm_scale
    raised = jnp.exp(3.0 * jnp.tanh(scores))
    number = iota((TABLE, DEVICES), 0).astype(f32)
    me = place[1] * 16 + place[0]
    mine = iota((1, DEVICES), 1) == me
    lane4 = iota((1, SLOTS), 1)
    summed = jnp.zeros((LANE, TABLE), f32)
    for n in range(2):
        group = raised[n * SLOTS : (n + 1) * SLOTS]
        share = group / jnp.sum(group, axis=0, keepdims=True)
        own = jnp.zeros((1, SLOTS), f32)
        table = jnp.zeros((TABLE, DEVICES), f32)
        for o in range(SLOTS):
            row = share[o : o + 1]
            asked = misc[n * SLOTS + o : n * SLOTS + o + 1, :]
            table = table + jnp.where(number == asked, row, 0.0)
            one = jnp.sum(jnp.where(mine, row, 0.0), axis=1, keepdims=True)
            own = jnp.where(lane4 == o, one, own)
        assignment[n : n + 1, :] = own
        summed = summed + dot(
            weighted[n * LANE : (n + 1) * LANE, :], table, ((1,), (1,)), lax.Precision.HIGHEST
        )
    for s in range(ROWS):
        chosen, inside, beyond = taps(lower, weight, s)
        rows = summed[s * 8 : (s + 1) * 8]
        at = pl.ds(s * TABLE, TABLE)
        for c in range(8):
            spreads[c * BLOCK : (c + 1) * BLOCK, at] = (rows[c : c + 1] * inside).astype(bf16)
        spreads[8 * BLOCK : 8 * BLOCK + 16, at] = jnp.concatenate(
            [rows * beyond, jnp.zeros((8, TABLE), f32)], axis=0
        ).astype(bf16)
        blocks[:, at] = chosen
    total = dot(spreads[...], blocks[...], ((1,), (1,)))
    carried = pltpu.roll(total[8 * BLOCK : 8 * BLOCK + 8], 1, 1)
    first = iota((BLOCK, DEVICES), 0) == 0
    accum = [
        total[c * BLOCK : (c + 1) * BLOCK] + jnp.where(first, carried[c : c + 1], 0.0) for c in range(8)
    ]
    ratio = misc[8:40, :]
    filtered = [accum[c] / (accum[FACTOR[c]] + ratio) for c in range(5)]
    wide[pl.ds(0, DEVICES, stride=2), :] = jnp.concatenate(filtered[:4], axis=0).T
    wide[pl.ds(1, DEVICES, stride=2), :] = jnp.concatenate(
        [filtered[4], jnp.zeros((LANE - BLOCK, DEVICES), f32)], axis=0
    ).T
    out[...] = wide[...].astype(bf16)


def field_kernel(got, table, out, wide):
    wide[...] = got[...].astype(f32)
    early = wide[pl.ds(0, DEVICES, stride=2), :].T
    late = wide[pl.ds(1, DEVICES, stride=2), :].T
    blocks = [early[c * BLOCK : (c + 1) * BLOCK] for c in range(4)] + [late[:BLOCK]]
    filtered = jnp.concatenate(blocks, axis=1).astype(bf16)
    out[...] = dot(filtered, table[...], ((1,), (0,)))


def whole():
    return pl.BlockSpec(memory_space=pltpu.VMEM)


def in_hbm(x):
    return pltpu.with_memory_space_constraint(x, pltpu.HBM)


def kernel_call(kernel, outs, scratch, in_specs):
    return pl.pallas_call(
        kernel,
        out_shape=outs,
        in_specs=in_specs,
        out_specs=jax.tree.map(lambda _: whole(), outs),
        scratch_shapes=scratch,
        compiler_params=pltpu.CompilerParams(vmem_limit_bytes=VMEM_LIMIT),
    )


def on_device(orientations, images, ctf_values, volume, line_index, line_weight, noise_ratio):
    img, vol = lax.axis_index("img"), lax.axis_index("vol")
    place = jnp.stack([img, vol]).astype(jnp.int32)
    norm_scale = 1.0 / math.sqrt(2.0 * ROWS * WIDTH)
    smem = pl.BlockSpec(memory_space=pltpu.SMEM)
    hbm = pl.BlockSpec(memory_space=pltpu.HBM)
    struct = jax.ShapeDtypeStruct
    message = kernel_call(
        pack_kernel,
        struct((4 * DEVICES, LANE), bf16),
        [
            pltpu.VMEM((BLOCK, 2 * WIDTH), bf16),
            pltpu.VMEM((BLOCK, WIDTH), bf16),
            pltpu.VMEM((BLOCK, 2 * WIDTH), bf16),
            pltpu.SMEM((SLOTS, BLOCK), jnp.int32),
            pltpu.SMEM((BLOCK,), f32),
            pltpu.VMEM((4 * DEVICES, LANE), f32),
            pltpu.SemaphoreType.DMA((5,)),
        ],
        [smem] + [hbm] * 5,
    )(
        place,
        in_hbm(images.reshape(BLOCK, 2 * WIDTH)),
        in_hbm(ctf_values.reshape(BLOCK, WIDTH)),
        in_hbm(volume),
        in_hbm(orientations.T),
        in_hbm(noise_ratio),
    )
    got = lax.all_to_all(message.reshape(DEVICES, 4, LANE), ORDER, 0, 0, tiled=True)
    part, weighted, misc, lower, weight = kernel_call(
        score_kernel,
        (
            struct((16, 8, DEVICES), f32),
            struct((DEVICES, DEVICES), f32),
            struct((40, DEVICES), f32),
            struct((ROWS, TABLE), jnp.int32),
            struct((ROWS, TABLE), f32),
        ),
        [pltpu.VMEM((4 * DEVICES, LANE), f32), pltpu.SemaphoreType.DMA((2,))],
        [whole(), hbm, hbm],
    )(got.reshape(4 * DEVICES, LANE), in_hbm(line_index.T), in_hbm(line_weight.T))
    part = lax.all_to_all(part, "img", 0, 0, tiled=True)
    part = kernel_call(relay_kernel, struct((16, 8, DEVICES), f32), [], [whole()])(part)
    part = lax.all_to_all(part, "vol", 0, 0, tiled=True)
    message, assignment = kernel_call(
        functools.partial(back_kernel, norm_scale=norm_scale),
        (struct((2 * DEVICES, LANE), bf16), struct((2, SLOTS), f32)),
        [
            pltpu.VMEM((8 * BLOCK + 16, ROWS * TABLE), bf16),
            pltpu.VMEM((DEVICES, ROWS * TABLE), bf16),
            pltpu.VMEM((2 * DEVICES, LANE), f32),
        ],
        [smem] + [whole()] * 5,
    )(place, part, weighted, misc, lower, weight)
    got = lax.all_to_all(message.reshape(DEVICES, 2, LANE), ORDER, 0, 0, tiled=True)
    density_map = kernel_call(
        field_kernel,
        struct((BLOCK, 2 * WIDTH), f32),
        [pltpu.VMEM((2 * DEVICES, LANE), f32)],
        [whole()] * 2,
    )(got.reshape(2 * DEVICES, LANE), jnp.asarray(inverse_rows()))
    return (assignment, density_map)


def solution(mesh):
    return jax.shard_map(
        on_device,
        mesh=mesh,
        in_specs=(
            P("img", None),
            P(("img", "vol"), None, None),
            P(("img", "vol"), None, None),
            P("vol", None),
            P(),
            P(),
            P(("vol", "img")),
        ),
        out_specs=(P(("img", "vol"), None), P(("vol", "img"), None)),
        check_vma=False,
    )
```

```python
import functools
import math

import jax
import jax.numpy as jnp
import numpy as np
from jax import lax
from jax.experimental import pallas as pl
from jax.experimental.pallas import tpu as pltpu
from jax.sharding import PartitionSpec as P

WIDTH = 640
ROWS = 16
TABLE = 256
SLOTS = 4
LINES = 8192
BANDS = ((0, 1, 4), (2, 3, 4))
LANE = 128
BLOCK = 32
DEVICES = 256
FACTOR = (5, 5, 6, 6, 7, 5, 6, 7)
ORDER = ("vol", "img")
VMEM_LIMIT = 48 * 1024 * 1024

f32 = jnp.float32
bf16 = jnp.bfloat16


def columns_of(half):
    first, second, last = BANDS[half]
    re = lambda band: LANE * band
    im = lambda band: WIDTH + LANE * band
    return (re(first), im(first), re(second), im(second), im(last) if half else re(last))


def inverse_rows():
    k = np.arange(WIDTH)
    angle = (np.outer(k, k) % WIDTH) * (2.0 * np.pi / WIDTH)
    table = np.concatenate([np.cos(angle), np.sin(angle)], 1) / np.sqrt(WIDTH)
    bands = (BANDS[0][0], BANDS[1][0], BANDS[0][1], BANDS[1][1], BANDS[0][2])
    rows = np.concatenate([np.arange(LANE * band, LANE * band + LANE) for band in bands])
    return np.asarray(table[rows], dtype=jnp.bfloat16)


def iota(shape, dim):
    return lax.broadcasted_iota(jnp.int32, shape, dim)


def dot(a, b, dims, precision=None):
    return lax.dot_general(a, b, (dims, ((), ())), precision=precision, preferred_element_type=f32)


def identity():
    return jnp.where(iota((LANE, LANE), 0) == iota((LANE, LANE), 1), 1.0, 0.0).astype(bf16)


def pack_kernel(
    place, images_in, ctf_in, volume_in, orientations_in, noise_in, out,
    images, ctf, volume, orientations, noise, mixed, wide, done,
):
    copies = [
        pltpu.make_async_copy(source, target, done.at[n])
        for n, (source, target) in enumerate(
            (
                (orientations_in, orientations),
                (noise_in, noise),
                (images_in, images),
                (ctf_in, ctf),
                (volume_in.at[pl.ds(pl.multiple_of(place[0] * BLOCK, BLOCK), BLOCK), :], volume),
            )
        )
    ]
    for copy in copies:
        copy.start()
    same = identity()
    for copy in copies:
        copy.wait()
    own = place[1] * 2
    row8 = iota((16, LANE), 0)
    asked = jnp.zeros((16, LANE), f32)
    for r in range(2 * SLOTS):
        value = orientations[r % SLOTS, own + r // SLOTS].astype(f32)
        asked = jnp.where(row8 == r, value, asked)
    row32 = iota((BLOCK, LANE), 0)
    ratio = jnp.zeros((BLOCK, LANE), f32)
    for r in range(BLOCK):
        ratio = jnp.where(row32 == r, noise[r], ratio)
    ratio_top = ratio.astype(bf16)
    ratio_rest = (ratio - ratio_top.astype(f32)).astype(bf16)
    common = [asked.astype(bf16), ratio_top, ratio_rest, jnp.zeros((16, LANE), bf16)]
    for half in range(2):
        starts = columns_of(half)
        pieces = [images[:, start : start + LANE] for start in starts]
        pieces += [ctf[:, LANE * band : LANE * band + LANE] for band in BANDS[half]]
        for c, piece in enumerate(pieces):
            piece = piece.astype(f32)
            for n in range(2):
                mixed[pl.ds(half * 256 + n * LANE + c, ROWS, stride=8), :] = piece[n * ROWS : (n + 1) * ROWS]
        others = jnp.concatenate([volume[:, start : start + LANE] for start in starts] + common, axis=0)
        left = dot(same, mixed[half * 256 : (half + 1) * 256, :].astype(bf16), ((1,), (1,)))
        right = dot(same, others, ((1,), (1,)))
        base = half * 4 * LANE
        wide[pl.ds(base, LANE, stride=4), :] = left[:, :LANE]
        wide[pl.ds(base + 1, LANE, stride=4), :] = left[:, LANE:]
        wide[pl.ds(base + 2, LANE, stride=4), :] = right[:, :LANE]
        wide[pl.ds(base + 3, LANE, stride=4), :] = right[:, LANE:]
    out[...] = wide[...].astype(bf16)


def taps(lower, weight, s):
    line = lower[s : s + 1, :]
    low = weight[s : s + 1, :]
    low_tap = low.astype(bf16).astype(f32)
    high_tap = (1.0 - low).astype(bf16).astype(f32)
    block = lax.shift_right_logical(line, 5)
    place = jnp.bitwise_and(line, BLOCK - 1)
    rows = iota((BLOCK, TABLE), 0)
    nothing = jnp.zeros((BLOCK, TABLE), f32)
    inside = jnp.where(rows == place, low_tap, jnp.where(rows == place + 1, high_tap, nothing))
    beyond = jnp.where(place == BLOCK - 1, high_tap, 0.0)
    chosen = jnp.where(iota((DEVICES, TABLE), 0).astype(jnp.int16) == block.astype(jnp.int16), jnp.ones((), bf16), jnp.zeros((), bf16))
    return chosen, inside, beyond


def score_kernel(got, line_index, line_weight, part, weighted, misc, lower, weight, wide, done):
    copies = [
        pltpu.make_async_copy(line_index, lower, done.at[0]),
        pltpu.make_async_copy(line_weight, weight, done.at[1]),
    ]
    for copy in copies:
        copy.start()
    wide[...] = got[...].astype(f32)
    quarter = [wide[pl.ds(a, DEVICES, stride=4), :].astype(bf16) for a in range(4)]
    to, frm = iota((LANE, LANE), 0), iota((LANE, LANE), 1)
    spread = jnp.zeros((LANE, LANE), f32)
    for c, factor in enumerate(FACTOR):
        spread = jnp.where((to % 8 == c) & (frm == to - c + factor), 1.0, spread)
    same = identity()
    both = jnp.concatenate([same, spread.astype(bf16)], axis=0)
    heavy = []
    for n in range(2):
        pair = dot(both, quarter[n], ((1,), (1,)))
        product = pair[:LANE] * pair[LANE:]
        weighted[n * LANE : (n + 1) * LANE, :] = product
        top = product.astype(bf16)
        rest = (product - top.astype(f32)).astype(bf16)
        heavy.append(jnp.concatenate([top, rest, top], axis=0))
    third = dot(same, quarter[2], ((1,), (1,)))
    fourth = dot(same, quarter[3], ((1,), (1,)))
    misc[0:8, :] = fourth[32:40, :]
    misc[8:40, :] = fourth[48:80, :] + fourth[80:112, :]
    lines = jnp.concatenate([third, fourth[:BLOCK]], axis=0)
    following = [pltpu.roll(lines[c * BLOCK : c * BLOCK + 8], DEVICES - 1, 1)[0:1] for c in range(5)]
    lines = jnp.concatenate([lines] + following + [jnp.zeros((11, DEVICES), f32)], axis=0).astype(bf16)
    for copy in copies:
        copy.wait()
    tables = []
    for s in range(ROWS):
        chosen, inside, beyond = taps(lower, weight, s)
        found = dot(lines, chosen, ((1,), (0,)))
        for c in range(5):
            tables.append(
                jnp.sum(found[c * BLOCK : (c + 1) * BLOCK] * inside, axis=0, keepdims=True)
                + found[5 * BLOCK + c : 5 * BLOCK + c + 1] * beyond
            )
        tables.append(jnp.zeros((3, TABLE), f32))
    slices = jnp.concatenate(tables, axis=0).T
    top = slices.astype(bf16)
    rest = (slices - top.astype(f32)).astype(bf16)
    slices = jnp.concatenate([top, top, rest], axis=1)
    number = iota((TABLE, DEVICES), 0).astype(f32)
    sums = []
    for n in range(2):
        products = dot(slices, heavy[n], ((1,), (0,)))
        for o in range(SLOTS):
            asked = misc[n * SLOTS + o : n * SLOTS + o + 1, :]
            sums.append(jnp.sum(jnp.where(number == asked, products, 0.0), axis=0, keepdims=True))
    part[...] = jnp.broadcast_to(jnp.concatenate(sums, axis=0)[None], part.shape)


def relay_kernel(got, out):
    out[...] = jnp.broadcast_to(jnp.sum(got[...], axis=0, keepdims=True), out.shape)


def back_kernel(place, got, weighted, misc, lower, weight, out, assignment, spreads, blocks, wide, norm_scale):
    scores = jnp.sum(got[...], axis=0) * norm_scale
    raised = jnp.exp(3.0 * jnp.tanh(scores))
    number = iota((TABLE, DEVICES), 0).astype(f32)
    me = place[1] * 16 + place[0]
    mine = iota((1, DEVICES), 1) == me
    lane4 = iota((1, SLOTS), 1)
    summed = jnp.zeros((LANE, TABLE), f32)
    for n in range(2):
        group = raised[n * SLOTS : (n + 1) * SLOTS]
        share = group / jnp.sum(group, axis=0, keepdims=True)
        own = jnp.zeros((1, SLOTS), f32)
        table = jnp.zeros((TABLE, DEVICES), f32)
        for o in range(SLOTS):
            row = share[o : o + 1]
            asked = misc[n * SLOTS + o : n * SLOTS + o + 1, :]
            table = table + jnp.where(number == asked, row, 0.0)
            one = jnp.sum(jnp.where(mine, row, 0.0), axis=1, keepdims=True)
            own = jnp.where(lane4 == o, one, own)
        assignment[n : n + 1, :] = own
        summed = summed + dot(
            weighted[n * LANE : (n + 1) * LANE, :].astype(bf16), table.astype(bf16), ((1,), (1,))
        )
    for s in range(ROWS):
        chosen, inside, beyond = taps(lower, weight, s)
        rows = summed[s * 8 : (s + 1) * 8]
        at = pl.ds(s * TABLE, TABLE)
        for c in range(8):
            spreads[c * BLOCK : (c + 1) * BLOCK, at] = (rows[c : c + 1] * inside).astype(bf16)
        spreads[8 * BLOCK : 8 * BLOCK + 16, at] = jnp.concatenate(
            [rows * beyond, jnp.zeros((8, TABLE), f32)], axis=0
        ).astype(bf16)
        blocks[:, at] = chosen
    total = dot(spreads[...], blocks[...], ((1,), (1,)))
    carried = pltpu.roll(total[8 * BLOCK : 8 * BLOCK + 8], 1, 1)
    first = iota((BLOCK, DEVICES), 0) == 0
    accum = [
        total[c * BLOCK : (c + 1) * BLOCK] + jnp.where(first, carried[c : c + 1], 0.0) for c in range(8)
    ]
    ratio = misc[8:40, :]
    filtered = [accum[c] / (accum[FACTOR[c]] + ratio) for c in range(5)]
    wide[pl.ds(0, DEVICES, stride=2), :] = jnp.concatenate(filtered[:4], axis=0).T
    wide[pl.ds(1, DEVICES, stride=2), :] = jnp.concatenate(
        [filtered[4], jnp.zeros((LANE - BLOCK, DEVICES), f32)], axis=0
    ).T
    out[...] = wide[...].astype(bf16)


def field_kernel(got, table, out, wide):
    wide[...] = got[...].astype(f32)
    early = wide[pl.ds(0, DEVICES, stride=2), :].T
    late = wide[pl.ds(1, DEVICES, stride=2), :].T[:BLOCK]
    block = [early[c * BLOCK : (c + 1) * BLOCK] for c in range(4)]
    real = jnp.concatenate([block[0], block[2], late[:, :LANE]], axis=1)
    imaginary = jnp.concatenate([block[1], block[3], late[:, LANE:]], axis=1)
    both = jnp.concatenate([real, imaginary], axis=0).astype(bf16)
    waves = dot(both, table[...], ((1,), (0,)))
    out[:, :WIDTH] = waves[:BLOCK, :WIDTH] - waves[BLOCK:, WIDTH:]
    out[:, WIDTH:] = waves[:BLOCK, WIDTH:] + waves[BLOCK:, :WIDTH]


def whole():
    return pl.BlockSpec(memory_space=pltpu.VMEM)


def in_hbm(x):
    return pltpu.with_memory_space_constraint(x, pltpu.HBM)


def kernel_call(kernel, outs, scratch, in_specs):
    return pl.pallas_call(
        kernel,
        out_shape=outs,
        in_specs=in_specs,
        out_specs=jax.tree.map(lambda _: whole(), outs),
        scratch_shapes=scratch,
        compiler_params=pltpu.CompilerParams(vmem_limit_bytes=VMEM_LIMIT),
    )


def on_device(orientations, images, ctf_values, volume, line_index, line_weight, noise_ratio):
    img, vol = lax.axis_index("img"), lax.axis_index("vol")
    place = jnp.stack([img, vol]).astype(jnp.int32)
    norm_scale = 1.0 / math.sqrt(2.0 * ROWS * WIDTH)
    smem = pl.BlockSpec(memory_space=pltpu.SMEM)
    hbm = pl.BlockSpec(memory_space=pltpu.HBM)
    struct = jax.ShapeDtypeStruct
    message = kernel_call(
        pack_kernel,
        struct((4 * DEVICES, LANE), bf16),
        [
            pltpu.VMEM((BLOCK, 2 * WIDTH), bf16),
            pltpu.VMEM((BLOCK, WIDTH), bf16),
            pltpu.VMEM((BLOCK, 2 * WIDTH), bf16),
            pltpu.SMEM((SLOTS, BLOCK), jnp.int32),
            pltpu.SMEM((BLOCK,), f32),
            pltpu.VMEM((512, LANE), f32),
            pltpu.VMEM((4 * DEVICES, LANE), f32),
            pltpu.SemaphoreType.DMA((5,)),
        ],
        [smem] + [hbm] * 5,
    )(
        place,
        in_hbm(images.reshape(BLOCK, 2 * WIDTH)),
        in_hbm(ctf_values.reshape(BLOCK, WIDTH)),
        in_hbm(volume),
        in_hbm(orientations.T),
        in_hbm(noise_ratio),
    )
    got = lax.all_to_all(message.reshape(DEVICES, 4, LANE), ORDER, 0, 0, tiled=True)
    part, weighted, misc, lower, weight = kernel_call(
        score_kernel,
        (
            struct((16, 8, DEVICES), f32),
            struct((DEVICES, DEVICES), f32),
            struct((40, DEVICES), f32),
            struct((ROWS, TABLE), jnp.int32),
            struct((ROWS, TABLE), f32),
        ),
        [pltpu.VMEM((4 * DEVICES, LANE), f32), pltpu.SemaphoreType.DMA((2,))],
        [whole(), hbm, hbm],
    )(got.reshape(4 * DEVICES, LANE), in_hbm(line_index.T), in_hbm(line_weight.T))
    part = lax.all_to_all(part, "img", 0, 0, tiled=True)
    part = kernel_call(relay_kernel, struct((16, 8, DEVICES), f32), [], [whole()])(part)
    part = lax.all_to_all(part, "vol", 0, 0, tiled=True)
    message, assignment = kernel_call(
        functools.partial(back_kernel, norm_scale=norm_scale),
        (struct((2 * DEVICES, LANE), bf16), struct((2, SLOTS), f32)),
        [
            pltpu.VMEM((8 * BLOCK + 16, ROWS * TABLE), bf16),
            pltpu.VMEM((DEVICES, ROWS * TABLE), bf16),
            pltpu.VMEM((2 * DEVICES, LANE), f32),
        ],
        [smem] + [whole()] * 5,
    )(place, part, weighted, misc, lower, weight)
    got = lax.all_to_all(message.reshape(DEVICES, 2, LANE), ORDER, 0, 0, tiled=True)
    density_map = kernel_call(
        field_kernel,
        struct((BLOCK, 2 * WIDTH), f32),
        [pltpu.VMEM((2 * DEVICES, LANE), f32)],
        [whole()] * 2,
    )(got.reshape(2 * DEVICES, LANE), jnp.asarray(inverse_rows()))
    return (assignment, density_map)


def solution(mesh):
    return jax.shard_map(
        on_device,
        mesh=mesh,
        in_specs=(
            P("img", None),
            P(("img", "vol"), None, None),
            P(("img", "vol"), None, None),
            P("vol", None),
            P(),
            P(),
            P(("vol", "img")),
        ),
        out_specs=(P(("img", "vol"), None), P(("vol", "img"), None)),
        check_vma=False,
    )
```

```python
import functools
import math

import jax
import jax.numpy as jnp
import numpy as np
from jax import lax
from jax.experimental import pallas as pl
from jax.experimental.pallas import tpu as pltpu
from jax.sharding import PartitionSpec as P

WIDTH = 640
ROWS = 16
TABLE = 256
SLOTS = 4
LINES = 8192
BANDS = ((0, 1, 4), (2, 3, 4))
LANE = 128
BLOCK = 32
DEVICES = 256
FACTOR = (5, 5, 6, 6, 7, 5, 6, 7)
ORDER = ("vol", "img")
VMEM_LIMIT = 48 * 1024 * 1024

f32 = jnp.float32
bf16 = jnp.bfloat16


def columns_of(half):
    first, second, last = BANDS[half]
    re = lambda band: LANE * band
    im = lambda band: WIDTH + LANE * band
    return (re(first), im(first), re(second), im(second), im(last) if half else re(last))


def inverse_rows():
    k = np.arange(WIDTH)
    angle = (np.outer(k, k) % WIDTH) * (2.0 * np.pi / WIDTH)
    table = np.concatenate([np.cos(angle), np.sin(angle)], 1) / np.sqrt(WIDTH)
    bands = (BANDS[0][0], BANDS[1][0], BANDS[0][1], BANDS[1][1], BANDS[0][2])
    rows = np.concatenate([np.arange(LANE * band, LANE * band + LANE) for band in bands])
    return np.asarray(table[rows], dtype=jnp.bfloat16)


def iota(shape, dim):
    return lax.broadcasted_iota(jnp.int32, shape, dim)


def dot(a, b, dims, precision=None):
    return lax.dot_general(a, b, (dims, ((), ())), precision=precision, preferred_element_type=f32)


def identity():
    return jnp.where(iota((LANE, LANE), 0) == iota((LANE, LANE), 1), 1.0, 0.0).astype(bf16)


def pack_kernel(
    images_in, ctf_in, volume_in, orientations_in, noise_in, index_in, weight_in, out, lower, weight,
    images, ctf, volume, orientations, noise, mixed, wide, done,
):
    copies = [
        pltpu.make_async_copy(source, target, done.at[n])
        for n, (source, target) in enumerate(
            (
                (orientations_in, orientations),
                (noise_in, noise),
                (index_in, lower),
                (weight_in, weight),
                (images_in, images),
                (ctf_in, ctf),
                (volume_in.at[pl.ds(pl.multiple_of(lax.axis_index("img") * BLOCK, BLOCK), BLOCK), :], volume),
            )
        )
    ]
    for copy in copies:
        copy.start()
    same = identity()
    for copy in copies:
        copy.wait()
    own = lax.axis_index("vol") * 2
    row8 = iota((16, LANE), 0)
    asked = jnp.zeros((16, LANE), f32)
    for r in range(2 * SLOTS):
        value = orientations[r % SLOTS, own + r // SLOTS].astype(f32)
        asked = jnp.where(row8 == r, value, asked)
    row32 = iota((BLOCK, LANE), 0)
    ratio = jnp.zeros((BLOCK, LANE), f32)
    for r in range(BLOCK):
        ratio = jnp.where(row32 == r, noise[r], ratio)
    ratio_top = ratio.astype(bf16)
    ratio_rest = (ratio - ratio_top.astype(f32)).astype(bf16)
    common = [asked.astype(bf16), ratio_top, ratio_rest, jnp.zeros((16, LANE), bf16)]
    for half in range(2):
        starts = columns_of(half)
        pieces = [images[:, start : start + LANE] for start in starts]
        pieces += [ctf[:, LANE * band : LANE * band + LANE] for band in BANDS[half]]
        for c, piece in enumerate(pieces):
            piece = piece.astype(f32)
            for n in range(2):
                mixed[pl.ds(half * 256 + n * LANE + c, ROWS, stride=8), :] = piece[n * ROWS : (n + 1) * ROWS]
        others = jnp.concatenate([volume[:, start : start + LANE] for start in starts] + common, axis=0)
        left = dot(same, mixed[half * 256 : (half + 1) * 256, :].astype(bf16), ((1,), (1,)))
        right = dot(same, others, ((1,), (1,)))
        base = half * 4 * LANE
        wide[pl.ds(base, LANE, stride=4), :] = left[:, :LANE]
        wide[pl.ds(base + 1, LANE, stride=4), :] = left[:, LANE:]
        wide[pl.ds(base + 2, LANE, stride=4), :] = right[:, :LANE]
        wide[pl.ds(base + 3, LANE, stride=4), :] = right[:, LANE:]
    out[...] = wide[...].astype(bf16)


def taps(lower, weight, s):
    line = lower[s : s + 1, :]
    low = weight[s : s + 1, :]
    low_tap = low.astype(bf16).astype(f32)
    high_tap = (1.0 - low).astype(bf16).astype(f32)
    block = lax.shift_right_logical(line, 5)
    place = jnp.bitwise_and(line, BLOCK - 1)
    rows = iota((BLOCK, TABLE), 0)
    nothing = jnp.zeros((BLOCK, TABLE), f32)
    inside = jnp.where(rows == place, low_tap, jnp.where(rows == place + 1, high_tap, nothing))
    beyond = jnp.where(place == BLOCK - 1, high_tap, 0.0)
    chosen = jnp.where(iota((DEVICES, TABLE), 0).astype(jnp.int16) == block.astype(jnp.int16), jnp.ones((), bf16), jnp.zeros((), bf16))
    return chosen, inside, beyond


def score_kernel(got, lower, weight, part, weighted, misc, wide):
    wide[...] = got[...].astype(f32)
    quarter = [wide[pl.ds(a, DEVICES, stride=4), :].astype(bf16) for a in range(4)]
    to, frm = iota((LANE, LANE), 0), iota((LANE, LANE), 1)
    spread = jnp.zeros((LANE, LANE), f32)
    for c, factor in enumerate(FACTOR):
        spread = jnp.where((to % 8 == c) & (frm == to - c + factor), 1.0, spread)
    same = identity()
    both = jnp.concatenate([same, spread.astype(bf16)], axis=0)
    heavy = []
    for n in range(2):
        pair = dot(both, quarter[n], ((1,), (1,)))
        product = pair[:LANE] * pair[LANE:]
        weighted[n * LANE : (n + 1) * LANE, :] = product
        top = product.astype(bf16)
        rest = (product - top.astype(f32)).astype(bf16)
        heavy.append(jnp.concatenate([top, rest, top], axis=0))
    third = dot(same, quarter[2], ((1,), (1,)))
    fourth = dot(same, quarter[3], ((1,), (1,)))
    misc[0:8, :] = fourth[32:40, :]
    misc[8:40, :] = fourth[48:80, :] + fourth[80:112, :]
    lines = jnp.concatenate([third, fourth[:BLOCK]], axis=0)
    following = [pltpu.roll(lines[c * BLOCK : c * BLOCK + 8], DEVICES - 1, 1)[0:1] for c in range(5)]
    lines = jnp.concatenate([lines] + following + [jnp.zeros((11, DEVICES), f32)], axis=0).astype(bf16)
    tables = []
    for s in range(ROWS):
        chosen, inside, beyond = taps(lower, weight, s)
        found = dot(lines, chosen, ((1,), (0,)))
        for c in range(5):
            tables.append(
                jnp.sum(found[c * BLOCK : (c + 1) * BLOCK] * inside, axis=0, keepdims=True)
                + found[5 * BLOCK + c : 5 * BLOCK + c + 1] * beyond
            )
        tables.append(jnp.zeros((3, TABLE), f32))
    slices = jnp.concatenate(tables, axis=0).T
    top = slices.astype(bf16)
    rest = (slices - top.astype(f32)).astype(bf16)
    slices = jnp.concatenate([top, top, rest], axis=1)
    number = iota((TABLE, DEVICES), 0).astype(f32)
    sums = []
    for n in range(2):
        products = dot(slices, heavy[n], ((1,), (0,)))
        for o in range(SLOTS):
            asked = misc[n * SLOTS + o : n * SLOTS + o + 1, :]
            sums.append(jnp.sum(jnp.where(number == asked, products, 0.0), axis=0, keepdims=True))
    part[...] = jnp.broadcast_to(jnp.concatenate(sums, axis=0)[None], part.shape)


def relay_kernel(got, out):
    out[...] = jnp.broadcast_to(jnp.sum(got[...], axis=0, keepdims=True), out.shape)


def back_kernel(got, weighted, misc, lower, weight, out, assignment, spreads, blocks, wide, norm_scale):
    scores = jnp.sum(got[...], axis=0) * norm_scale
    raised = jnp.exp(3.0 * jnp.tanh(scores))
    number = iota((TABLE, DEVICES), 0).astype(f32)
    me = lax.axis_index("vol") * 16 + lax.axis_index("img")
    mine = iota((1, DEVICES), 1) == me
    lane4 = iota((1, SLOTS), 1)
    summed = jnp.zeros((LANE, TABLE), f32)
    for n in range(2):
        group = raised[n * SLOTS : (n + 1) * SLOTS]
        share = group / jnp.sum(group, axis=0, keepdims=True)
        own = jnp.zeros((1, SLOTS), f32)
        table = jnp.zeros((TABLE, DEVICES), f32)
        for o in range(SLOTS):
            row = share[o : o + 1]
            asked = misc[n * SLOTS + o : n * SLOTS + o + 1, :]
            table = table + jnp.where(number == asked, row, 0.0)
            one = jnp.sum(jnp.where(mine, row, 0.0), axis=1, keepdims=True)
            own = jnp.where(lane4 == o, one, own)
        assignment[n : n + 1, :] = own
        summed = summed + dot(
            weighted[n * LANE : (n + 1) * LANE, :].astype(bf16), table.astype(bf16), ((1,), (1,))
        )
    for s in range(ROWS):
        chosen, inside, beyond = taps(lower, weight, s)
        rows = summed[s * 8 : (s + 1) * 8]
        at = pl.ds(s * TABLE, TABLE)
        for c in range(8):
            spreads[c * BLOCK : (c + 1) * BLOCK, at] = (rows[c : c + 1] * inside).astype(bf16)
        spreads[8 * BLOCK : 8 * BLOCK + 16, at] = jnp.concatenate(
            [rows * beyond, jnp.zeros((8, TABLE), f32)], axis=0
        ).astype(bf16)
        blocks[:, at] = chosen
    total = dot(spreads[...], blocks[...], ((1,), (1,)))
    carried = pltpu.roll(total[8 * BLOCK : 8 * BLOCK + 8], 1, 1)
    first = iota((BLOCK, DEVICES), 0) == 0
    accum = [
        total[c * BLOCK : (c + 1) * BLOCK] + jnp.where(first, carried[c : c + 1], 0.0) for c in range(8)
    ]
    ratio = misc[8:40, :]
    filtered = [accum[c] / (accum[FACTOR[c]] + ratio) for c in range(5)]
    wide[pl.ds(0, DEVICES, stride=2), :] = jnp.concatenate(filtered[:4], axis=0).T
    wide[pl.ds(1, DEVICES, stride=2), :] = jnp.concatenate(
        [filtered[4], jnp.zeros((LANE - BLOCK, DEVICES), f32)], axis=0
    ).T
    out[...] = wide[...].astype(bf16)


def field_kernel(got, table, out, wide):
    wide[...] = got[...].astype(f32)
    early = wide[pl.ds(0, DEVICES, stride=2), :].T
    late = wide[pl.ds(1, DEVICES, stride=2), :].T[:BLOCK]
    block = [early[c * BLOCK : (c + 1) * BLOCK] for c in range(4)]
    real = jnp.concatenate([block[0], block[2], late[:, :LANE]], axis=1)
    imaginary = jnp.concatenate([block[1], block[3], late[:, LANE:]], axis=1)
    both = jnp.concatenate([real, imaginary], axis=0).astype(bf16)
    waves = dot(both, table[...], ((1,), (0,)))
    out[:, :WIDTH] = waves[:BLOCK, :WIDTH] - waves[BLOCK:, WIDTH:]
    out[:, WIDTH:] = waves[:BLOCK, WIDTH:] + waves[BLOCK:, :WIDTH]


def whole():
    return pl.BlockSpec(memory_space=pltpu.VMEM)


def in_hbm(x):
    return pltpu.with_memory_space_constraint(x, pltpu.HBM)


def kernel_call(kernel, outs, scratch, in_specs):
    return pl.pallas_call(
        kernel,
        out_shape=outs,
        in_specs=in_specs,
        out_specs=jax.tree.map(lambda _: whole(), outs),
        scratch_shapes=scratch,
        compiler_params=pltpu.CompilerParams(vmem_limit_bytes=VMEM_LIMIT),
    )


def on_device(orientations, images, ctf_values, volume, line_index, line_weight, noise_ratio):
    norm_scale = 1.0 / math.sqrt(2.0 * ROWS * WIDTH)
    hbm = pl.BlockSpec(memory_space=pltpu.HBM)
    struct = jax.ShapeDtypeStruct
    message, lower, weight = kernel_call(
        pack_kernel,
        (
            struct((4 * DEVICES, LANE), bf16),
            struct((ROWS, TABLE), jnp.int32),
            struct((ROWS, TABLE), f32),
        ),
        [
            pltpu.VMEM((BLOCK, 2 * WIDTH), bf16),
            pltpu.VMEM((BLOCK, WIDTH), bf16),
            pltpu.VMEM((BLOCK, 2 * WIDTH), bf16),
            pltpu.SMEM((SLOTS, BLOCK), jnp.int32),
            pltpu.SMEM((BLOCK,), f32),
            pltpu.VMEM((512, LANE), f32),
            pltpu.VMEM((4 * DEVICES, LANE), f32),
            pltpu.SemaphoreType.DMA((7,)),
        ],
        [hbm] * 7,
    )(
        in_hbm(images.reshape(BLOCK, 2 * WIDTH)),
        in_hbm(ctf_values.reshape(BLOCK, WIDTH)),
        in_hbm(volume),
        in_hbm(orientations.T),
        in_hbm(noise_ratio),
        in_hbm(line_index.T),
        in_hbm(line_weight.T),
    )
    got = lax.all_to_all(message.reshape(DEVICES, 4, LANE), ORDER, 0, 0, tiled=True)
    part, weighted, misc = kernel_call(
        score_kernel,
        (
            struct((16, 8, DEVICES), f32),
            struct((DEVICES, DEVICES), f32),
            struct((40, DEVICES), f32),
        ),
        [pltpu.VMEM((4 * DEVICES, LANE), f32)],
        [whole()] * 3,
    )(got.reshape(4 * DEVICES, LANE), lower, weight)
    part = lax.all_to_all(part, "img", 0, 0, tiled=True)
    part = kernel_call(relay_kernel, struct((16, 8, DEVICES), f32), [], [whole()])(part)
    part = lax.all_to_all(part, "vol", 0, 0, tiled=True)
    message, assignment = kernel_call(
        functools.partial(back_kernel, norm_scale=norm_scale),
        (struct((2 * DEVICES, LANE), bf16), struct((2, SLOTS), f32)),
        [
            pltpu.VMEM((8 * BLOCK + 16, ROWS * TABLE), bf16),
            pltpu.VMEM((DEVICES, ROWS * TABLE), bf16),
            pltpu.VMEM((2 * DEVICES, LANE), f32),
        ],
        [whole()] * 5,
    )(part, weighted, misc, lower, weight)
    got = lax.all_to_all(message.reshape(DEVICES, 2, LANE), ORDER, 0, 0, tiled=True)
    density_map = kernel_call(
        field_kernel,
        struct((BLOCK, 2 * WIDTH), f32),
        [pltpu.VMEM((2 * DEVICES, LANE), f32)],
        [whole()] * 2,
    )(got.reshape(2 * DEVICES, LANE), jnp.asarray(inverse_rows()))
    return (assignment, density_map)


def solution(mesh):
    return jax.shard_map(
        on_device,
        mesh=mesh,
        in_specs=(
            P("img", None),
            P(("img", "vol"), None, None),
            P(("img", "vol"), None, None),
            P("vol", None),
            P(),
            P(),
            P(("vol", "img")),
        ),
        out_specs=(P(("img", "vol"), None), P(("vol", "img"), None)),
        check_vma=False,
    )
```

```python
import functools
import math

import jax
import jax.numpy as jnp
import numpy as np
from jax import lax
from jax.experimental import pallas as pl
from jax.experimental.pallas import tpu as pltpu
from jax.sharding import PartitionSpec as P

WIDTH = 640
ROWS = 16
TABLE = 256
SLOTS = 4
LINES = 8192
BANDS = ((0, 1, 4), (2, 3, 4))
LANE = 128
BLOCK = 32
DEVICES = 256
FACTOR = (5, 5, 6, 6, 7, 5, 6, 7)
ORDER = ("vol", "img")
VMEM_LIMIT = 48 * 1024 * 1024

f32 = jnp.float32
bf16 = jnp.bfloat16


def columns_of(half):
    first, second, last = BANDS[half]
    re = lambda band: LANE * band
    im = lambda band: WIDTH + LANE * band
    return (re(first), im(first), re(second), im(second), im(last) if half else re(last))


def inverse_rows():
    k = np.arange(WIDTH)
    angle = (np.outer(k, k) % WIDTH) * (2.0 * np.pi / WIDTH)
    table = np.concatenate([np.cos(angle), np.sin(angle)], 1) / np.sqrt(WIDTH)
    bands = (BANDS[0][0], BANDS[1][0], BANDS[0][1], BANDS[1][1], BANDS[0][2])
    rows = np.concatenate([np.arange(LANE * band, LANE * band + LANE) for band in bands])
    return np.asarray(table[rows], dtype=jnp.bfloat16)


def iota(shape, dim):
    return lax.broadcasted_iota(jnp.int32, shape, dim)


def dot(a, b, dims, precision=None):
    return lax.dot_general(a, b, (dims, ((), ())), precision=precision, preferred_element_type=f32)


def identity():
    return jnp.where(iota((LANE, LANE), 0) == iota((LANE, LANE), 1), 1.0, 0.0).astype(bf16)


def pack_kernel(
    images_in, ctf_in, volume_in, orientations_in, noise_in, index_in, weight_in, out, lower, weight,
    images, ctf, volume, orientations, noise, mixed, wide, done,
):
    copies = [
        pltpu.make_async_copy(source, target, done.at[n])
        for n, (source, target) in enumerate(
            (
                (orientations_in, orientations),
                (noise_in, noise),
                (index_in, lower),
                (weight_in, weight),
                (images_in, images),
                (ctf_in, ctf),
                (volume_in.at[pl.ds(pl.multiple_of(lax.axis_index("img") * BLOCK, BLOCK), BLOCK), :], volume),
            )
        )
    ]
    for copy in copies:
        copy.start()
    same = identity()
    for copy in copies:
        copy.wait()
    own = lax.axis_index("vol") * 2
    row8 = iota((16, LANE), 0)
    asked = jnp.zeros((16, LANE), f32)
    for r in range(2 * SLOTS):
        value = orientations[r % SLOTS, own + r // SLOTS].astype(f32)
        asked = jnp.where(row8 == r, value, asked)
    row32 = iota((BLOCK, LANE), 0)
    ratio = jnp.zeros((BLOCK, LANE), f32)
    for r in range(BLOCK):
        ratio = jnp.where(row32 == r, noise[r], ratio)
    ratio_top = ratio.astype(bf16)
    ratio_rest = (ratio - ratio_top.astype(f32)).astype(bf16)
    common = [asked.astype(bf16), ratio_top, ratio_rest, jnp.zeros((16, LANE), bf16)]
    for half in range(2):
        starts = columns_of(half)
        pieces = [images[:, start : start + LANE] for start in starts]
        pieces += [ctf[:, LANE * band : LANE * band + LANE] for band in BANDS[half]]
        for c, piece in enumerate(pieces):
            piece = piece.astype(f32)
            for n in range(2):
                mixed[pl.ds(half * 256 + n * LANE + c, ROWS, stride=8), :] = piece[n * ROWS : (n + 1) * ROWS]
        others = jnp.concatenate([volume[:, start : start + LANE] for start in starts] + common, axis=0)
        left = dot(same, mixed[half * 256 : (half + 1) * 256, :].astype(bf16), ((1,), (1,)))
        right = dot(same, others, ((1,), (1,)))
        base = half * 4 * LANE
        wide[pl.ds(base, LANE, stride=4), :] = left[:, :LANE]
        wide[pl.ds(base + 1, LANE, stride=4), :] = left[:, LANE:]
        wide[pl.ds(base + 2, LANE, stride=4), :] = right[:, :LANE]
        wide[pl.ds(base + 3, LANE, stride=4), :] = right[:, LANE:]
    out[...] = wide[...].astype(bf16)


def taps(lower, weight, s):
    line = lower[s : s + 1, :]
    low = weight[s : s + 1, :]
    low_tap = low.astype(bf16).astype(f32)
    high_tap = (1.0 - low).astype(bf16).astype(f32)
    block = lax.shift_right_logical(line, 5)
    place = jnp.bitwise_and(line, BLOCK - 1)
    rows = iota((BLOCK, TABLE), 0)
    nothing = jnp.zeros((BLOCK, TABLE), f32)
    inside = jnp.where(rows == place, low_tap, jnp.where(rows == place + 1, high_tap, nothing))
    beyond = jnp.where(place == BLOCK - 1, high_tap, 0.0)
    chosen = jnp.where(iota((DEVICES, TABLE), 0).astype(jnp.int16) == block.astype(jnp.int16), jnp.ones((), bf16), jnp.zeros((), bf16))
    return chosen, inside, beyond


def score_kernel(got, lower, weight, table_in, part, weighted, misc, table, wide, done):
    fetch = pltpu.make_async_copy(table_in, table, done)
    fetch.start()
    wide[...] = got[...].astype(f32)
    quarter = [wide[pl.ds(a, DEVICES, stride=4), :].astype(bf16) for a in range(4)]
    to, frm = iota((LANE, LANE), 0), iota((LANE, LANE), 1)
    spread = jnp.zeros((LANE, LANE), f32)
    for c, factor in enumerate(FACTOR):
        spread = jnp.where((to % 8 == c) & (frm == to - c + factor), 1.0, spread)
    same = identity()
    both = jnp.concatenate([same, spread.astype(bf16)], axis=0)
    heavy = []
    for n in range(2):
        pair = dot(both, quarter[n], ((1,), (1,)))
        product = pair[:LANE] * pair[LANE:]
        weighted[n * LANE : (n + 1) * LANE, :] = product
        top = product.astype(bf16)
        rest = (product - top.astype(f32)).astype(bf16)
        heavy.append(jnp.concatenate([top, rest, top], axis=0))
    third = dot(same, quarter[2], ((1,), (1,)))
    fourth = dot(same, quarter[3], ((1,), (1,)))
    misc[0:8, :] = fourth[32:40, :]
    misc[8:40, :] = fourth[48:80, :] + fourth[80:112, :]
    lines = jnp.concatenate([third, fourth[:BLOCK]], axis=0)
    following = [pltpu.roll(lines[c * BLOCK : c * BLOCK + 8], DEVICES - 1, 1)[0:1] for c in range(5)]
    lines = jnp.concatenate([lines] + following + [jnp.zeros((11, DEVICES), f32)], axis=0).astype(bf16)
    tables = []
    for s in range(ROWS):
        chosen, inside, beyond = taps(lower, weight, s)
        found = dot(lines, chosen, ((1,), (0,)))
        for c in range(5):
            tables.append(
                jnp.sum(found[c * BLOCK : (c + 1) * BLOCK] * inside, axis=0, keepdims=True)
                + found[5 * BLOCK + c : 5 * BLOCK + c + 1] * beyond
            )
        tables.append(jnp.zeros((3, TABLE), f32))
    slices = jnp.concatenate(tables, axis=0).T
    top = slices.astype(bf16)
    rest = (slices - top.astype(f32)).astype(bf16)
    slices = jnp.concatenate([top, top, rest], axis=1)
    number = iota((TABLE, DEVICES), 0).astype(f32)
    sums = []
    for n in range(2):
        products = dot(slices, heavy[n], ((1,), (0,)))
        for o in range(SLOTS):
            asked = misc[n * SLOTS + o : n * SLOTS + o + 1, :]
            sums.append(jnp.sum(jnp.where(number == asked, products, 0.0), axis=0, keepdims=True))
    part[...] = jnp.broadcast_to(jnp.concatenate(sums, axis=0)[None], part.shape)
    fetch.wait()


def relay_kernel(got, out):
    out[...] = jnp.broadcast_to(jnp.sum(got[...], axis=0, keepdims=True), out.shape)


def back_kernel(got, weighted, misc, lower, weight, out, assignment, spreads, blocks, wide, norm_scale):
    scores = jnp.sum(got[...], axis=0) * norm_scale
    raised = jnp.exp(3.0 * jnp.tanh(scores))
    number = iota((TABLE, DEVICES), 0).astype(f32)
    me = lax.axis_index("vol") * 16 + lax.axis_index("img")
    mine = iota((1, DEVICES), 1) == me
    lane4 = iota((1, SLOTS), 1)
    summed = jnp.zeros((LANE, TABLE), f32)
    for n in range(2):
        group = raised[n * SLOTS : (n + 1) * SLOTS]
        share = group / jnp.sum(group, axis=0, keepdims=True)
        own = jnp.zeros((1, SLOTS), f32)
        table = jnp.zeros((TABLE, DEVICES), f32)
        for o in range(SLOTS):
            row = share[o : o + 1]
            asked = misc[n * SLOTS + o : n * SLOTS + o + 1, :]
            table = table + jnp.where(number == asked, row, 0.0)
            one = jnp.sum(jnp.where(mine, row, 0.0), axis=1, keepdims=True)
            own = jnp.where(lane4 == o, one, own)
        assignment[n : n + 1, :] = own
        summed = summed + dot(
            weighted[n * LANE : (n + 1) * LANE, :].astype(bf16), table.astype(bf16), ((1,), (1,))
        )
    for s in range(ROWS):
        chosen, inside, beyond = taps(lower, weight, s)
        rows = summed[s * 8 : (s + 1) * 8]
        at = pl.ds(s * TABLE, TABLE)
        for c in range(8):
            spreads[c * BLOCK : (c + 1) * BLOCK, at] = (rows[c : c + 1] * inside).astype(bf16)
        spreads[8 * BLOCK : 8 * BLOCK + 16, at] = jnp.concatenate(
            [rows * beyond, jnp.zeros((8, TABLE), f32)], axis=0
        ).astype(bf16)
        blocks[:, at] = chosen
    total = dot(spreads[...], blocks[...], ((1,), (1,)))
    carried = pltpu.roll(total[8 * BLOCK : 8 * BLOCK + 8], 1, 1)
    first = iota((BLOCK, DEVICES), 0) == 0
    accum = [
        total[c * BLOCK : (c + 1) * BLOCK] + jnp.where(first, carried[c : c + 1], 0.0) for c in range(8)
    ]
    ratio = misc[8:40, :]
    filtered = [accum[c] / (accum[FACTOR[c]] + ratio) for c in range(5)]
    wide[pl.ds(0, DEVICES, stride=2), :] = jnp.concatenate(filtered[:4], axis=0).T
    wide[pl.ds(1, DEVICES, stride=2), :] = jnp.concatenate(
        [filtered[4], jnp.zeros((LANE - BLOCK, DEVICES), f32)], axis=0
    ).T
    out[...] = wide[...].astype(bf16)


def field_kernel(got, table, out, wide):
    wide[...] = got[...].astype(f32)
    early = wide[pl.ds(0, DEVICES, stride=2), :].T
    late = wide[pl.ds(1, DEVICES, stride=2), :].T[:BLOCK]
    block = [early[c * BLOCK : (c + 1) * BLOCK] for c in range(4)]
    real = jnp.concatenate([block[0], block[2], late[:, :LANE]], axis=1)
    imaginary = jnp.concatenate([block[1], block[3], late[:, LANE:]], axis=1)
    both = jnp.concatenate([real, imaginary], axis=0).astype(bf16)
    waves = dot(both, table[...], ((1,), (0,)))
    out[:, :WIDTH] = waves[:BLOCK, :WIDTH] - waves[BLOCK:, WIDTH:]
    out[:, WIDTH:] = waves[:BLOCK, WIDTH:] + waves[BLOCK:, :WIDTH]


def whole():
    return pl.BlockSpec(memory_space=pltpu.VMEM)


def in_hbm(x):
    return pltpu.with_memory_space_constraint(x, pltpu.HBM)


def kernel_call(kernel, outs, scratch, in_specs):
    return pl.pallas_call(
        kernel,
        out_shape=outs,
        in_specs=in_specs,
        out_specs=jax.tree.map(lambda _: whole(), outs),
        scratch_shapes=scratch,
        compiler_params=pltpu.CompilerParams(vmem_limit_bytes=VMEM_LIMIT),
    )


def on_device(orientations, images, ctf_values, volume, line_index, line_weight, noise_ratio):
    norm_scale = 1.0 / math.sqrt(2.0 * ROWS * WIDTH)
    hbm = pl.BlockSpec(memory_space=pltpu.HBM)
    struct = jax.ShapeDtypeStruct
    message, lower, weight = kernel_call(
        pack_kernel,
        (
            struct((4 * DEVICES, LANE), bf16),
            struct((ROWS, TABLE), jnp.int32),
            struct((ROWS, TABLE), f32),
        ),
        [
            pltpu.VMEM((BLOCK, 2 * WIDTH), bf16),
            pltpu.VMEM((BLOCK, WIDTH), bf16),
            pltpu.VMEM((BLOCK, 2 * WIDTH), bf16),
            pltpu.SMEM((SLOTS, BLOCK), jnp.int32),
            pltpu.SMEM((BLOCK,), f32),
            pltpu.VMEM((512, LANE), f32),
            pltpu.VMEM((4 * DEVICES, LANE), f32),
            pltpu.SemaphoreType.DMA((7,)),
        ],
        [hbm] * 7,
    )(
        in_hbm(images.reshape(BLOCK, 2 * WIDTH)),
        in_hbm(ctf_values.reshape(BLOCK, WIDTH)),
        in_hbm(volume),
        in_hbm(orientations.T),
        in_hbm(noise_ratio),
        in_hbm(line_index.T),
        in_hbm(line_weight.T),
    )
    got = lax.all_to_all(message.reshape(DEVICES, 4, LANE), ORDER, 0, 0, tiled=True)
    part, weighted, misc, table = kernel_call(
        score_kernel,
        (
            struct((16, 8, DEVICES), f32),
            struct((DEVICES, DEVICES), f32),
            struct((40, DEVICES), f32),
            struct((WIDTH, 2 * WIDTH), bf16),
        ),
        [pltpu.VMEM((4 * DEVICES, LANE), f32), pltpu.SemaphoreType.DMA],
        [whole()] * 3 + [hbm],
    )(got.reshape(4 * DEVICES, LANE), lower, weight, in_hbm(jnp.asarray(inverse_rows())))
    part = lax.all_to_all(part, "vol", 0, 0, tiled=True)
    part = kernel_call(relay_kernel, struct((16, 8, DEVICES), f32), [], [whole()])(part)
    part = lax.all_to_all(part, "img", 0, 0, tiled=True)
    message, assignment = kernel_call(
        functools.partial(back_kernel, norm_scale=norm_scale),
        (struct((2 * DEVICES, LANE), bf16), struct((2, SLOTS), f32)),
        [
            pltpu.VMEM((8 * BLOCK + 16, ROWS * TABLE), bf16),
            pltpu.VMEM((DEVICES, ROWS * TABLE), bf16),
            pltpu.VMEM((2 * DEVICES, LANE), f32),
        ],
        [whole()] * 5,
    )(part, weighted, misc, lower, weight)
    got = lax.all_to_all(message.reshape(DEVICES, 2, LANE), ORDER, 0, 0, tiled=True)
    density_map = kernel_call(
        field_kernel,
        struct((BLOCK, 2 * WIDTH), f32),
        [pltpu.VMEM((2 * DEVICES, LANE), f32)],
        [whole()] * 2,
    )(got.reshape(2 * DEVICES, LANE), table)
    return (assignment, density_map)


def solution(mesh):
    return jax.shard_map(
        on_device,
        mesh=mesh,
        in_specs=(
            P("img", None),
            P(("img", "vol"), None, None),
            P(("img", "vol"), None, None),
            P("vol", None),
            P(),
            P(),
            P(("vol", "img")),
        ),
        out_specs=(P(("img", "vol"), None), P(("vol", "img"), None)),
        check_vma=False,
    )
```

```python
import functools
import math

import jax
import jax.numpy as jnp
import numpy as np
from jax import lax
from jax.experimental import pallas as pl
from jax.experimental.pallas import tpu as pltpu
from jax.sharding import PartitionSpec as P

WIDTH = 640
ROWS = 16
TABLE = 256
SLOTS = 4
LINES = 8192
BANDS = ((0, 1, 4), (2, 3, 4))
LANE = 128
BLOCK = 32
DEVICES = 256
FACTOR = (5, 5, 6, 6, 7, 5, 6, 7)
ORDER = ("vol", "img")
FLAT = [[(8 * xh + 2 * y + c) * 16 + 8 * xl + z for xl in range(2) for xh in range(2) for y in range(4)] for z in range(8) for c in range(2)]
DEEP = [[(8 * xh + 2 * y + c) * 16 + 8 * xl + z for z in range(8) for c in range(2)] for xl in range(2) for xh in range(2) for y in range(4)]
VMEM_LIMIT = 48 * 1024 * 1024

f32 = jnp.float32
bf16 = jnp.bfloat16


def columns_of(half):
    first, second, last = BANDS[half]
    re = lambda band: LANE * band
    im = lambda band: WIDTH + LANE * band
    return (re(first), im(first), re(second), im(second), im(last) if half else re(last))


def inverse_rows():
    k = np.arange(WIDTH)
    angle = (np.outer(k, k) % WIDTH) * (2.0 * np.pi / WIDTH)
    table = np.concatenate([np.cos(angle), np.sin(angle)], 1) / np.sqrt(WIDTH)
    bands = (BANDS[0][0], BANDS[1][0], BANDS[0][1], BANDS[1][1], BANDS[0][2])
    rows = np.concatenate([np.arange(LANE * band, LANE * band + LANE) for band in bands])
    return np.asarray(table[rows], dtype=jnp.bfloat16)


def iota(shape, dim):
    return lax.broadcasted_iota(jnp.int32, shape, dim)


def dot(a, b, dims, precision=None):
    return lax.dot_general(a, b, (dims, ((), ())), precision=precision, preferred_element_type=f32)


def identity():
    return jnp.where(iota((LANE, LANE), 0) == iota((LANE, LANE), 1), 1.0, 0.0).astype(bf16)


def pack_kernel(
    images_in, ctf_in, volume_in, orientations_in, noise_in, index_in, weight_in, out, lower, weight,
    images, ctf, volume, orientations, noise, mixed, wide, done,
):
    copies = [
        pltpu.make_async_copy(source, target, done.at[n])
        for n, (source, target) in enumerate(
            (
                (orientations_in, orientations),
                (noise_in, noise),
                (index_in, lower),
                (weight_in, weight),
                (images_in, images),
                (ctf_in, ctf),
                (volume_in.at[pl.ds(pl.multiple_of(lax.axis_index("img") * BLOCK, BLOCK), BLOCK), :], volume),
            )
        )
    ]
    for copy in copies:
        copy.start()
    same = identity()
    for copy in copies:
        copy.wait()
    own = lax.axis_index("vol") * 2
    row8 = iota((16, LANE), 0)
    asked = jnp.zeros((16, LANE), f32)
    for r in range(2 * SLOTS):
        value = orientations[r % SLOTS, own + r // SLOTS].astype(f32)
        asked = jnp.where(row8 == r, value, asked)
    row32 = iota((BLOCK, LANE), 0)
    ratio = jnp.zeros((BLOCK, LANE), f32)
    for r in range(BLOCK):
        ratio = jnp.where(row32 == r, noise[r], ratio)
    ratio_top = ratio.astype(bf16)
    ratio_rest = (ratio - ratio_top.astype(f32)).astype(bf16)
    common = [asked.astype(bf16), ratio_top, ratio_rest, jnp.zeros((16, LANE), bf16)]
    for half in range(2):
        starts = columns_of(half)
        pieces = [images[:, start : start + LANE] for start in starts]
        pieces += [ctf[:, LANE * band : LANE * band + LANE] for band in BANDS[half]]
        for c, piece in enumerate(pieces):
            piece = piece.astype(f32)
            for n in range(2):
                mixed[pl.ds(half * 256 + n * LANE + c, ROWS, stride=8), :] = piece[n * ROWS : (n + 1) * ROWS]
        others = jnp.concatenate([volume[:, start : start + LANE] for start in starts] + common, axis=0)
        left = dot(same, mixed[half * 256 : (half + 1) * 256, :].astype(bf16), ((1,), (1,)))
        right = dot(same, others, ((1,), (1,)))
        base = half * 4 * LANE
        wide[pl.ds(base, LANE, stride=4), :] = left[:, :LANE]
        wide[pl.ds(base + 1, LANE, stride=4), :] = left[:, LANE:]
        wide[pl.ds(base + 2, LANE, stride=4), :] = right[:, :LANE]
        wide[pl.ds(base + 3, LANE, stride=4), :] = right[:, LANE:]
    out[...] = wide[...].astype(bf16)


def taps(lower, weight, s):
    line = lower[s : s + 1, :]
    low = weight[s : s + 1, :]
    low_tap = low.astype(bf16).astype(f32)
    high_tap = (1.0 - low).astype(bf16).astype(f32)
    block = lax.shift_right_logical(line, 5)
    place = jnp.bitwise_and(line, BLOCK - 1)
    rows = iota((BLOCK, TABLE), 0)
    nothing = jnp.zeros((BLOCK, TABLE), f32)
    inside = jnp.where(rows == place, low_tap, jnp.where(rows == place + 1, high_tap, nothing))
    beyond = jnp.where(place == BLOCK - 1, high_tap, 0.0)
    chosen = jnp.where(iota((DEVICES, TABLE), 0).astype(jnp.int16) == block.astype(jnp.int16), jnp.ones((), bf16), jnp.zeros((), bf16))
    return chosen, inside, beyond


def score_kernel(got, lower, weight, table_in, part, weighted, misc, table, wide, done):
    fetch = pltpu.make_async_copy(table_in, table, done)
    fetch.start()
    wide[...] = got[...].astype(f32)
    quarter = [wide[pl.ds(a, DEVICES, stride=4), :].astype(bf16) for a in range(4)]
    to, frm = iota((LANE, LANE), 0), iota((LANE, LANE), 1)
    spread = jnp.zeros((LANE, LANE), f32)
    for c, factor in enumerate(FACTOR):
        spread = jnp.where((to % 8 == c) & (frm == to - c + factor), 1.0, spread)
    same = identity()
    both = jnp.concatenate([same, spread.astype(bf16)], axis=0)
    heavy = []
    for n in range(2):
        pair = dot(both, quarter[n], ((1,), (1,)))
        product = pair[:LANE] * pair[LANE:]
        weighted[n * LANE : (n + 1) * LANE, :] = product
        top = product.astype(bf16)
        rest = (product - top.astype(f32)).astype(bf16)
        heavy.append(jnp.concatenate([top, rest, top], axis=0))
    third = dot(same, quarter[2], ((1,), (1,)))
    fourth = dot(same, quarter[3], ((1,), (1,)))
    misc[0:8, :] = fourth[32:40, :]
    misc[8:40, :] = fourth[48:80, :] + fourth[80:112, :]
    lines = jnp.concatenate([third, fourth[:BLOCK]], axis=0)
    following = [pltpu.roll(lines[c * BLOCK : c * BLOCK + 8], DEVICES - 1, 1)[0:1] for c in range(5)]
    lines = jnp.concatenate([lines] + following + [jnp.zeros((11, DEVICES), f32)], axis=0).astype(bf16)
    tables = []
    for s in range(ROWS):
        chosen, inside, beyond = taps(lower, weight, s)
        found = dot(lines, chosen, ((1,), (0,)))
        for c in range(5):
            tables.append(
                jnp.sum(found[c * BLOCK : (c + 1) * BLOCK] * inside, axis=0, keepdims=True)
                + found[5 * BLOCK + c : 5 * BLOCK + c + 1] * beyond
            )
        tables.append(jnp.zeros((3, TABLE), f32))
    slices = jnp.concatenate(tables, axis=0).T
    top = slices.astype(bf16)
    rest = (slices - top.astype(f32)).astype(bf16)
    slices = jnp.concatenate([top, top, rest], axis=1)
    number = iota((TABLE, DEVICES), 0).astype(f32)
    sums = []
    for n in range(2):
        products = dot(slices, heavy[n], ((1,), (0,)))
        for o in range(SLOTS):
            asked = misc[n * SLOTS + o : n * SLOTS + o + 1, :]
            sums.append(jnp.sum(jnp.where(number == asked, products, 0.0), axis=0, keepdims=True))
    part[...] = jnp.broadcast_to(jnp.concatenate(sums, axis=0)[None], part.shape)
    fetch.wait()


def relay_kernel(got, out):
    out[...] = jnp.broadcast_to(jnp.sum(got[...], axis=0, keepdims=True), out.shape)


def back_kernel(got, weighted, misc, lower, weight, out, assignment, spreads, blocks, wide, norm_scale):
    scores = jnp.sum(got[...], axis=0) * norm_scale
    raised = jnp.exp(3.0 * jnp.tanh(scores))
    number = iota((TABLE, DEVICES), 0).astype(f32)
    me = lax.axis_index("vol") * 16 + lax.axis_index("img")
    mine = iota((1, DEVICES), 1) == me
    lane4 = iota((1, SLOTS), 1)
    summed = jnp.zeros((LANE, TABLE), f32)
    for n in range(2):
        group = raised[n * SLOTS : (n + 1) * SLOTS]
        share = group / jnp.sum(group, axis=0, keepdims=True)
        own = jnp.zeros((1, SLOTS), f32)
        table = jnp.zeros((TABLE, DEVICES), f32)
        for o in range(SLOTS):
            row = share[o : o + 1]
            asked = misc[n * SLOTS + o : n * SLOTS + o + 1, :]
            table = table + jnp.where(number == asked, row, 0.0)
            one = jnp.sum(jnp.where(mine, row, 0.0), axis=1, keepdims=True)
            own = jnp.where(lane4 == o, one, own)
        assignment[n : n + 1, :] = own
        summed = summed + dot(
            weighted[n * LANE : (n + 1) * LANE, :].astype(bf16), table.astype(bf16), ((1,), (1,))
        )
    for s in range(ROWS):
        chosen, inside, beyond = taps(lower, weight, s)
        rows = summed[s * 8 : (s + 1) * 8]
        at = pl.ds(s * TABLE, TABLE)
        for c in range(8):
            spreads[c * BLOCK : (c + 1) * BLOCK, at] = (rows[c : c + 1] * inside).astype(bf16)
        spreads[8 * BLOCK : 8 * BLOCK + 16, at] = jnp.concatenate(
            [rows * beyond, jnp.zeros((8, TABLE), f32)], axis=0
        ).astype(bf16)
        blocks[:, at] = chosen
    total = dot(spreads[...], blocks[...], ((1,), (1,)))
    carried = pltpu.roll(total[8 * BLOCK : 8 * BLOCK + 8], 1, 1)
    first = iota((BLOCK, DEVICES), 0) == 0
    accum = [
        total[c * BLOCK : (c + 1) * BLOCK] + jnp.where(first, carried[c : c + 1], 0.0) for c in range(8)
    ]
    ratio = misc[8:40, :]
    filtered = [accum[c] / (accum[FACTOR[c]] + ratio) for c in range(5)]
    wide[pl.ds(0, DEVICES, stride=2), :] = jnp.concatenate(filtered[:4], axis=0).T
    wide[pl.ds(1, DEVICES, stride=2), :] = jnp.concatenate(
        [filtered[4], jnp.zeros((LANE - BLOCK, DEVICES), f32)], axis=0
    ).T
    out[...] = wide[...].astype(bf16)


def field_kernel(got, table, out, wide):
    wide[...] = got[...].astype(f32)
    early = wide[pl.ds(0, DEVICES, stride=2), :].T
    late = wide[pl.ds(1, DEVICES, stride=2), :].T[:BLOCK]
    block = [early[c * BLOCK : (c + 1) * BLOCK] for c in range(4)]
    real = jnp.concatenate([block[0], block[2], late[:, :LANE]], axis=1)
    imaginary = jnp.concatenate([block[1], block[3], late[:, LANE:]], axis=1)
    both = jnp.concatenate([real, imaginary], axis=0).astype(bf16)
    waves = dot(both, table[...], ((1,), (0,)))
    out[:, :WIDTH] = waves[:BLOCK, :WIDTH] - waves[BLOCK:, WIDTH:]
    out[:, WIDTH:] = waves[:BLOCK, WIDTH:] + waves[BLOCK:, :WIDTH]


def whole():
    return pl.BlockSpec(memory_space=pltpu.VMEM)


def in_hbm(x):
    return pltpu.with_memory_space_constraint(x, pltpu.HBM)


def kernel_call(kernel, outs, scratch, in_specs):
    return pl.pallas_call(
        kernel,
        out_shape=outs,
        in_specs=in_specs,
        out_specs=jax.tree.map(lambda _: whole(), outs),
        scratch_shapes=scratch,
        compiler_params=pltpu.CompilerParams(vmem_limit_bytes=VMEM_LIMIT),
    )


def on_device(orientations, images, ctf_values, volume, line_index, line_weight, noise_ratio):
    norm_scale = 1.0 / math.sqrt(2.0 * ROWS * WIDTH)
    hbm = pl.BlockSpec(memory_space=pltpu.HBM)
    struct = jax.ShapeDtypeStruct
    message, lower, weight = kernel_call(
        pack_kernel,
        (
            struct((4 * DEVICES, LANE), bf16),
            struct((ROWS, TABLE), jnp.int32),
            struct((ROWS, TABLE), f32),
        ),
        [
            pltpu.VMEM((BLOCK, 2 * WIDTH), bf16),
            pltpu.VMEM((BLOCK, WIDTH), bf16),
            pltpu.VMEM((BLOCK, 2 * WIDTH), bf16),
            pltpu.SMEM((SLOTS, BLOCK), jnp.int32),
            pltpu.SMEM((BLOCK,), f32),
            pltpu.VMEM((512, LANE), f32),
            pltpu.VMEM((4 * DEVICES, LANE), f32),
            pltpu.SemaphoreType.DMA((7,)),
        ],
        [hbm] * 7,
    )(
        in_hbm(images.reshape(BLOCK, 2 * WIDTH)),
        in_hbm(ctf_values.reshape(BLOCK, WIDTH)),
        in_hbm(volume),
        in_hbm(orientations.T),
        in_hbm(noise_ratio),
        in_hbm(line_index.T),
        in_hbm(line_weight.T),
    )
    got = lax.all_to_all(message.reshape(DEVICES, 4, LANE), ORDER, 0, 0, tiled=True)
    part, weighted, misc, table = kernel_call(
        score_kernel,
        (
            struct((16, 8, DEVICES), f32),
            struct((DEVICES, DEVICES), f32),
            struct((40, DEVICES), f32),
            struct((WIDTH, 2 * WIDTH), bf16),
        ),
        [pltpu.VMEM((4 * DEVICES, LANE), f32), pltpu.SemaphoreType.DMA],
        [whole()] * 3 + [hbm],
    )(got.reshape(4 * DEVICES, LANE), lower, weight, in_hbm(jnp.asarray(inverse_rows())))
    part = lax.all_to_all(part, ORDER, 0, 0, axis_index_groups=FLAT, tiled=True)
    part = kernel_call(relay_kernel, struct((16, 8, DEVICES), f32), [], [whole()])(part)
    part = lax.all_to_all(part, ORDER, 0, 0, axis_index_groups=DEEP, tiled=True)
    message, assignment = kernel_call(
        functools.partial(back_kernel, norm_scale=norm_scale),
        (struct((2 * DEVICES, LANE), bf16), struct((2, SLOTS), f32)),
        [
            pltpu.VMEM((8 * BLOCK + 16, ROWS * TABLE), bf16),
            pltpu.VMEM((DEVICES, ROWS * TABLE), bf16),
            pltpu.VMEM((2 * DEVICES, LANE), f32),
        ],
        [whole()] * 5,
    )(part, weighted, misc, lower, weight)
    got = lax.all_to_all(message.reshape(DEVICES, 2, LANE), ORDER, 0, 0, tiled=True)
    density_map = kernel_call(
        field_kernel,
        struct((BLOCK, 2 * WIDTH), f32),
        [pltpu.VMEM((2 * DEVICES, LANE), f32)],
        [whole()] * 2,
    )(got.reshape(2 * DEVICES, LANE), table)
    return (assignment, density_map)


def solution(mesh):
    return jax.shard_map(
        on_device,
        mesh=mesh,
        in_specs=(
            P("img", None),
            P(("img", "vol"), None, None),
            P(("img", "vol"), None, None),
            P("vol", None),
            P(),
            P(),
            P(("vol", "img")),
        ),
        out_specs=(P(("img", "vol"), None), P(("vol", "img"), None)),
        check_vma=False,
    )
```

```python
import functools
import math

import jax
import jax.numpy as jnp
import numpy as np
from jax import lax
from jax.experimental import pallas as pl
from jax.experimental.pallas import tpu as pltpu
from jax.sharding import PartitionSpec as P

WIDTH = 640
ROWS = 16
TABLE = 256
SLOTS = 4
LINES = 8192
BANDS = ((0, 1, 4), (2, 3, 4))
LANE = 128
BLOCK = 32
DEVICES = 256
FACTOR = (5, 5, 6, 6, 7, 5, 6, 7)
ORDER = ("img", "vol")
OTHER_ORDER = ("vol", "img")
FLAT = [[(8 * xh + 2 * y + c) * 16 + 8 * xl + z for xl in range(2) for xh in range(2) for y in range(4)] for z in range(8) for c in range(2)]
DEEP = [[(8 * xh + 2 * y + c) * 16 + 8 * xl + z for z in range(8) for c in range(2)] for xl in range(2) for xh in range(2) for y in range(4)]
VMEM_LIMIT = 48 * 1024 * 1024

f32 = jnp.float32
bf16 = jnp.bfloat16


def columns_of(half):
    first, second, last = BANDS[half]
    re = lambda band: LANE * band
    im = lambda band: WIDTH + LANE * band
    return (re(first), im(first), re(second), im(second), im(last) if half else re(last))


def inverse_rows():
    k = np.arange(WIDTH)
    angle = (np.outer(k, k) % WIDTH) * (2.0 * np.pi / WIDTH)
    table = np.concatenate([np.cos(angle), np.sin(angle)], 1) / np.sqrt(WIDTH)
    bands = (BANDS[0][0], BANDS[1][0], BANDS[0][1], BANDS[1][1], BANDS[0][2])
    rows = np.concatenate([np.arange(LANE * band, LANE * band + LANE) for band in bands])
    return np.asarray(table[rows], dtype=jnp.bfloat16)


def iota(shape, dim):
    return lax.broadcasted_iota(jnp.int32, shape, dim)


def dot(a, b, dims, precision=None):
    return lax.dot_general(a, b, (dims, ((), ())), precision=precision, preferred_element_type=f32)


def identity():
    return jnp.where(iota((LANE, LANE), 0) == iota((LANE, LANE), 1), 1.0, 0.0).astype(bf16)


def pack_kernel(
    images_in, ctf_in, volume_in, orientations_in, noise_in, index_in, weight_in, out, lower, weight,
    images, ctf, volume, orientations, noise, mixed, wide, done,
):
    copies = [
        pltpu.make_async_copy(source, target, done.at[n])
        for n, (source, target) in enumerate(
            (
                (orientations_in, orientations),
                (noise_in, noise),
                (index_in, lower),
                (weight_in, weight),
                (images_in, images),
                (ctf_in, ctf),
                (volume_in.at[pl.ds(pl.multiple_of(lax.axis_index("img") * BLOCK, BLOCK), BLOCK), :], volume),
            )
        )
    ]
    for copy in copies:
        copy.start()
    same = identity()
    for copy in copies:
        copy.wait()
    own = lax.axis_index("vol") * 2
    row8 = iota((16, LANE), 0)
    asked = jnp.zeros((16, LANE), f32)
    for r in range(2 * SLOTS):
        value = orientations[r % SLOTS, own + r // SLOTS].astype(f32)
        asked = jnp.where(row8 == r, value, asked)
    row32 = iota((BLOCK, LANE), 0)
    ratio = jnp.zeros((BLOCK, LANE), f32)
    for r in range(BLOCK):
        ratio = jnp.where(row32 == r, noise[r], ratio)
    ratio_top = ratio.astype(bf16)
    ratio_rest = (ratio - ratio_top.astype(f32)).astype(bf16)
    common = [asked.astype(bf16), ratio_top, ratio_rest, jnp.zeros((16, LANE), bf16)]
    for half in range(2):
        starts = columns_of(half)
        pieces = [images[:, start : start + LANE] for start in starts]
        pieces += [ctf[:, LANE * band : LANE * band + LANE] for band in BANDS[half]]
        for c, piece in enumerate(pieces):
            piece = piece.astype(f32)
            for n in range(2):
                mixed[pl.ds(half * 256 + n * LANE + c, ROWS, stride=8), :] = piece[n * ROWS : (n + 1) * ROWS]
        others = jnp.concatenate([volume[:, start : start + LANE] for start in starts] + common, axis=0)
        left = dot(same, mixed[half * 256 : (half + 1) * 256, :].astype(bf16), ((1,), (1,)))
        right = dot(same, others, ((1,), (1,)))
        base = half * 4 * LANE
        wide[pl.ds(base, LANE, stride=4), :] = left[:, :LANE]
        wide[pl.ds(base + 1, LANE, stride=4), :] = left[:, LANE:]
        wide[pl.ds(base + 2, LANE, stride=4), :] = right[:, :LANE]
        wide[pl.ds(base + 3, LANE, stride=4), :] = right[:, LANE:]
    out[...] = wide[...].astype(bf16)


def taps(lower, weight, s):
    line = lower[s : s + 1, :]
    low = weight[s : s + 1, :]
    low_tap = low.astype(bf16).astype(f32)
    high_tap = (1.0 - low).astype(bf16).astype(f32)
    block = jnp.bitwise_and(lax.shift_right_logical(line, 5), 15) * 16 + lax.shift_right_logical(line, 9)
    place = jnp.bitwise_and(line, BLOCK - 1)
    rows = iota((BLOCK, TABLE), 0)
    nothing = jnp.zeros((BLOCK, TABLE), f32)
    inside = jnp.where(rows == place, low_tap, jnp.where(rows == place + 1, high_tap, nothing))
    beyond = jnp.where(place == BLOCK - 1, high_tap, 0.0)
    chosen = jnp.where(iota((DEVICES, TABLE), 0).astype(jnp.int16) == block.astype(jnp.int16), jnp.ones((), bf16), jnp.zeros((), bf16))
    return chosen, inside, beyond


def score_kernel(got, lower, weight, table_in, part, weighted, misc, table, wide, done):
    fetch = pltpu.make_async_copy(table_in, table, done)
    fetch.start()
    wide[...] = got[...].astype(f32)
    quarter = [wide[pl.ds(a, DEVICES, stride=4), :].astype(bf16) for a in range(4)]
    to, frm = iota((LANE, LANE), 0), iota((LANE, LANE), 1)
    spread = jnp.zeros((LANE, LANE), f32)
    for c, factor in enumerate(FACTOR):
        spread = jnp.where((to % 8 == c) & (frm == to - c + factor), 1.0, spread)
    same = identity()
    both = jnp.concatenate([same, spread.astype(bf16)], axis=0)
    heavy = []
    for n in range(2):
        pair = dot(both, quarter[n], ((1,), (1,)))
        product = pair[:LANE] * pair[LANE:]
        weighted[n * LANE : (n + 1) * LANE, :] = product
        top = product.astype(bf16)
        rest = (product - top.astype(f32)).astype(bf16)
        heavy.append(jnp.concatenate([top, rest, top], axis=0))
    third = dot(same, quarter[2], ((1,), (1,)))
    fourth = dot(same, quarter[3], ((1,), (1,)))
    misc[0:8, :] = fourth[32:40, :]
    misc[8:40, :] = fourth[48:80, :] + fourth[80:112, :]
    lines = jnp.concatenate([third, fourth[:BLOCK]], axis=0)
    first = [lines[c * BLOCK : c * BLOCK + 1] for c in range(5)] + [jnp.zeros((3, DEVICES), f32)]
    near = pltpu.roll(jnp.concatenate(first, axis=0), DEVICES - 16, 1)
    at = iota((8, DEVICES), 1)
    across = jnp.where(at < DEVICES - 1, pltpu.roll(near, DEVICES - 1, 1), pltpu.roll(near, 15, 1))
    following = jnp.where(at < DEVICES - 16, near, across)
    lines = jnp.concatenate([lines, following, jnp.zeros((8, DEVICES), f32)], axis=0).astype(bf16)
    tables = []
    for s in range(ROWS):
        chosen, inside, beyond = taps(lower, weight, s)
        found = dot(lines, chosen, ((1,), (0,)))
        for c in range(5):
            tables.append(
                jnp.sum(found[c * BLOCK : (c + 1) * BLOCK] * inside, axis=0, keepdims=True)
                + found[5 * BLOCK + c : 5 * BLOCK + c + 1] * beyond
            )
        tables.append(jnp.zeros((3, TABLE), f32))
    slices = jnp.concatenate(tables, axis=0).T
    top = slices.astype(bf16)
    rest = (slices - top.astype(f32)).astype(bf16)
    slices = jnp.concatenate([top, top, rest], axis=1)
    number = iota((TABLE, DEVICES), 0).astype(f32)
    sums = []
    for n in range(2):
        products = dot(slices, heavy[n], ((1,), (0,)))
        for o in range(SLOTS):
            asked = misc[n * SLOTS + o : n * SLOTS + o + 1, :]
            sums.append(jnp.sum(jnp.where(number == asked, products, 0.0), axis=0, keepdims=True))
    part[...] = jnp.broadcast_to(jnp.concatenate(sums, axis=0)[None], part.shape)
    fetch.wait()


def relay_kernel(got, out):
    out[...] = jnp.broadcast_to(jnp.sum(got[...], axis=0, keepdims=True), out.shape)


def back_kernel(got, weighted, misc, lower, weight, out, assignment, spreads, blocks, wide, norm_scale):
    scores = jnp.sum(got[...], axis=0) * norm_scale
    raised = jnp.exp(3.0 * jnp.tanh(scores))
    number = iota((TABLE, DEVICES), 0).astype(f32)
    me = lax.axis_index("img") * 16 + lax.axis_index("vol")
    mine = iota((1, DEVICES), 1) == me
    lane4 = iota((1, SLOTS), 1)
    summed = jnp.zeros((LANE, TABLE), f32)
    for n in range(2):
        group = raised[n * SLOTS : (n + 1) * SLOTS]
        share = group / jnp.sum(group, axis=0, keepdims=True)
        own = jnp.zeros((1, SLOTS), f32)
        table = jnp.zeros((TABLE, DEVICES), f32)
        for o in range(SLOTS):
            row = share[o : o + 1]
            asked = misc[n * SLOTS + o : n * SLOTS + o + 1, :]
            table = table + jnp.where(number == asked, row, 0.0)
            one = jnp.sum(jnp.where(mine, row, 0.0), axis=1, keepdims=True)
            own = jnp.where(lane4 == o, one, own)
        assignment[n : n + 1, :] = own
        summed = summed + dot(
            weighted[n * LANE : (n + 1) * LANE, :].astype(bf16), table.astype(bf16), ((1,), (1,))
        )
    for s in range(ROWS):
        chosen, inside, beyond = taps(lower, weight, s)
        rows = summed[s * 8 : (s + 1) * 8]
        at = pl.ds(s * TABLE, TABLE)
        for c in range(8):
            spreads[c * BLOCK : (c + 1) * BLOCK, at] = (rows[c : c + 1] * inside).astype(bf16)
        spreads[8 * BLOCK : 8 * BLOCK + 16, at] = jnp.concatenate(
            [rows * beyond, jnp.zeros((8, TABLE), f32)], axis=0
        ).astype(bf16)
        blocks[:, at] = chosen
    total = dot(spreads[...], blocks[...], ((1,), (1,)))
    near = pltpu.roll(total[8 * BLOCK : 8 * BLOCK + 8], 16, 1)
    at = iota((8, DEVICES), 1)
    across = jnp.where(at >= 1, pltpu.roll(near, 1, 1), pltpu.roll(near, DEVICES - 15, 1))
    carried = jnp.where(at >= 16, near, across)
    first = iota((BLOCK, DEVICES), 0) == 0
    accum = [
        total[c * BLOCK : (c + 1) * BLOCK] + jnp.where(first, carried[c : c + 1], 0.0) for c in range(8)
    ]
    ratio = misc[8:40, :]
    filtered = [accum[c] / (accum[FACTOR[c]] + ratio) for c in range(5)]
    wide[pl.ds(0, DEVICES, stride=2), :] = jnp.concatenate(filtered[:4], axis=0).T
    wide[pl.ds(1, DEVICES, stride=2), :] = jnp.concatenate(
        [filtered[4], jnp.zeros((LANE - BLOCK, DEVICES), f32)], axis=0
    ).T
    out[...] = wide[...].astype(bf16)


def field_kernel(got, table, out, wide):
    wide[...] = got[...].astype(f32)
    early = wide[pl.ds(0, DEVICES, stride=2), :].T
    late = wide[pl.ds(1, DEVICES, stride=2), :].T[:BLOCK]
    block = [early[c * BLOCK : (c + 1) * BLOCK] for c in range(4)]
    real = jnp.concatenate([block[0], block[2], late[:, :LANE]], axis=1)
    imaginary = jnp.concatenate([block[1], block[3], late[:, LANE:]], axis=1)
    both = jnp.concatenate([real, imaginary], axis=0).astype(bf16)
    waves = dot(both, table[...], ((1,), (0,)))
    out[:, :WIDTH] = waves[:BLOCK, :WIDTH] - waves[BLOCK:, WIDTH:]
    out[:, WIDTH:] = waves[:BLOCK, WIDTH:] + waves[BLOCK:, :WIDTH]


def whole():
    return pl.BlockSpec(memory_space=pltpu.VMEM)


def in_hbm(x):
    return pltpu.with_memory_space_constraint(x, pltpu.HBM)


def kernel_call(kernel, outs, scratch, in_specs):
    return pl.pallas_call(
        kernel,
        out_shape=outs,
        in_specs=in_specs,
        out_specs=jax.tree.map(lambda _: whole(), outs),
        scratch_shapes=scratch,
        compiler_params=pltpu.CompilerParams(vmem_limit_bytes=VMEM_LIMIT),
    )


def on_device(orientations, images, ctf_values, volume, line_index, line_weight, noise_ratio):
    norm_scale = 1.0 / math.sqrt(2.0 * ROWS * WIDTH)
    hbm = pl.BlockSpec(memory_space=pltpu.HBM)
    struct = jax.ShapeDtypeStruct
    message, lower, weight = kernel_call(
        pack_kernel,
        (
            struct((4 * DEVICES, LANE), bf16),
            struct((ROWS, TABLE), jnp.int32),
            struct((ROWS, TABLE), f32),
        ),
        [
            pltpu.VMEM((BLOCK, 2 * WIDTH), bf16),
            pltpu.VMEM((BLOCK, WIDTH), bf16),
            pltpu.VMEM((BLOCK, 2 * WIDTH), bf16),
            pltpu.SMEM((SLOTS, BLOCK), jnp.int32),
            pltpu.SMEM((BLOCK,), f32),
            pltpu.VMEM((512, LANE), f32),
            pltpu.VMEM((4 * DEVICES, LANE), f32),
            pltpu.SemaphoreType.DMA((7,)),
        ],
        [hbm] * 7,
    )(
        in_hbm(images.reshape(BLOCK, 2 * WIDTH)),
        in_hbm(ctf_values.reshape(BLOCK, WIDTH)),
        in_hbm(volume),
        in_hbm(orientations.T),
        in_hbm(noise_ratio),
        in_hbm(line_index.T),
        in_hbm(line_weight.T),
    )
    got = lax.all_to_all(message.reshape(DEVICES, 4, LANE), ORDER, 0, 0, tiled=True)
    part, weighted, misc, table = kernel_call(
        score_kernel,
        (
            struct((16, 8, DEVICES), f32),
            struct((DEVICES, DEVICES), f32),
            struct((40, DEVICES), f32),
            struct((WIDTH, 2 * WIDTH), bf16),
        ),
        [pltpu.VMEM((4 * DEVICES, LANE), f32), pltpu.SemaphoreType.DMA],
        [whole()] * 3 + [hbm],
    )(got.reshape(4 * DEVICES, LANE), lower, weight, in_hbm(jnp.asarray(inverse_rows())))
    part = lax.all_to_all(part, OTHER_ORDER, 0, 0, axis_index_groups=FLAT, tiled=True)
    part = kernel_call(relay_kernel, struct((16, 8, DEVICES), f32), [], [whole()])(part)
    part = lax.all_to_all(part, OTHER_ORDER, 0, 0, axis_index_groups=DEEP, tiled=True)
    message, assignment = kernel_call(
        functools.partial(back_kernel, norm_scale=norm_scale),
        (struct((2 * DEVICES, LANE), bf16), struct((2, SLOTS), f32)),
        [
            pltpu.VMEM((8 * BLOCK + 16, ROWS * TABLE), bf16),
            pltpu.VMEM((DEVICES, ROWS * TABLE), bf16),
            pltpu.VMEM((2 * DEVICES, LANE), f32),
        ],
        [whole()] * 5,
    )(part, weighted, misc, lower, weight)
    got = lax.all_to_all(message.reshape(DEVICES, 2, LANE), ORDER, 0, 0, tiled=True)
    density_map = kernel_call(
        field_kernel,
        struct((BLOCK, 2 * WIDTH), f32),
        [pltpu.VMEM((2 * DEVICES, LANE), f32)],
        [whole()] * 2,
    )(got.reshape(2 * DEVICES, LANE), table)
    return (assignment, density_map)


def solution(mesh):
    return jax.shard_map(
        on_device,
        mesh=mesh,
        in_specs=(
            P("img", None),
            P(("img", "vol"), None, None),
            P(("img", "vol"), None, None),
            P("vol", None),
            P(),
            P(),
            P(("vol", "img")),
        ),
        out_specs=(P(("img", "vol"), None), P(("vol", "img"), None)),
        check_vma=False,
    )
```

```python
import functools
import math

import jax
import jax.numpy as jnp
import numpy as np
from jax import lax
from jax.experimental import pallas as pl
from jax.experimental.pallas import tpu as pltpu
from jax.sharding import PartitionSpec as P

WIDTH = 640
ROWS = 16
TABLE = 256
SLOTS = 4
LINES = 8192
BANDS = ((0, 1, 4), (2, 3, 4))
LANE = 128
BLOCK = 32
DEVICES = 256
FACTOR = (5, 5, 6, 6, 7, 5, 6, 7)
ORDER = ("img", "vol")
OTHER_ORDER = ("vol", "img")
FLAT = [[(8 * xh + 2 * y + c) * 16 + 8 * xl + z for xl in range(2) for xh in range(2) for y in range(4)] for z in range(8) for c in range(2)]
DEEP = [[(8 * xh + 2 * y + c) * 16 + 8 * xl + z for z in range(8) for c in range(2)] for xl in range(2) for xh in range(2) for y in range(4)]
VMEM_LIMIT = 48 * 1024 * 1024

f32 = jnp.float32
bf16 = jnp.bfloat16


def columns_of(half):
    first, second, last = BANDS[half]
    re = lambda band: LANE * band
    im = lambda band: WIDTH + LANE * band
    return (re(first), im(first), re(second), im(second), im(last) if half else re(last))


def inverse_rows():
    k = np.arange(WIDTH)
    angle = (np.outer(k, k) % WIDTH) * (2.0 * np.pi / WIDTH)
    table = np.concatenate([np.cos(angle), np.sin(angle)], 1) / np.sqrt(WIDTH)
    bands = (BANDS[0][0], BANDS[1][0], BANDS[0][1], BANDS[1][1], BANDS[0][2])
    rows = np.concatenate([np.arange(LANE * band, LANE * band + LANE) for band in bands])
    return np.asarray(table[rows], dtype=jnp.bfloat16)


def iota(shape, dim):
    return lax.broadcasted_iota(jnp.int32, shape, dim)


def dot(a, b, dims, precision=None):
    return lax.dot_general(a, b, (dims, ((), ())), precision=precision, preferred_element_type=f32)


def identity():
    return jnp.where(iota((LANE, LANE), 0) == iota((LANE, LANE), 1), 1.0, 0.0).astype(bf16)


def pack_kernel(
    images_in, ctf_in, volume_in, orientations_in, noise_in, index_in, weight_in, out, lower, weight,
    images, ctf, volume, orientations, noise, mixed, wide, done,
):
    copies = [
        pltpu.make_async_copy(source, target, done.at[n])
        for n, (source, target) in enumerate(
            (
                (orientations_in, orientations),
                (noise_in, noise),
                (index_in, lower),
                (weight_in, weight),
                (images_in, images),
                (ctf_in, ctf),
                (volume_in.at[pl.ds(pl.multiple_of(lax.axis_index("img") * BLOCK, BLOCK), BLOCK), :], volume),
            )
        )
    ]
    for copy in copies:
        copy.start()
    same = identity()
    for copy in copies:
        copy.wait()
    own = lax.axis_index("vol") * 2
    row8 = iota((16, LANE), 0)
    asked = jnp.zeros((16, LANE), f32)
    for r in range(2 * SLOTS):
        value = orientations[r % SLOTS, own + r // SLOTS].astype(f32)
        asked = jnp.where(row8 == r, value, asked)
    row32 = iota((BLOCK, LANE), 0)
    ratio = jnp.zeros((BLOCK, LANE), f32)
    for r in range(BLOCK):
        ratio = jnp.where(row32 == r, noise[r], ratio)
    ratio_top = ratio.astype(bf16)
    ratio_rest = (ratio - ratio_top.astype(f32)).astype(bf16)
    common = [asked.astype(bf16), ratio_top, ratio_rest, jnp.zeros((16, LANE), bf16)]
    for half in range(2):
        starts = columns_of(half)
        pieces = [images[:, start : start + LANE] for start in starts]
        pieces += [ctf[:, LANE * band : LANE * band + LANE] for band in BANDS[half]]
        for c, piece in enumerate(pieces):
            piece = piece.astype(f32)
            for n in range(2):
                mixed[pl.ds(half * 256 + n * LANE + c, ROWS, stride=8), :] = piece[n * ROWS : (n + 1) * ROWS]
        others = jnp.concatenate([volume[:, start : start + LANE] for start in starts] + common, axis=0)
        left = dot(same, mixed[half * 256 : (half + 1) * 256, :].astype(bf16), ((1,), (1,)))
        right = dot(same, others, ((1,), (1,)))
        base = half * 4 * LANE
        wide[pl.ds(base, LANE, stride=4), :] = left[:, :LANE]
        wide[pl.ds(base + 1, LANE, stride=4), :] = left[:, LANE:]
        wide[pl.ds(base + 2, LANE, stride=4), :] = right[:, :LANE]
        wide[pl.ds(base + 3, LANE, stride=4), :] = right[:, LANE:]
    out[...] = wide[...].astype(bf16)


def taps(lower, weight, s):
    line = lower[s : s + 1, :]
    low = weight[s : s + 1, :]
    low_tap = low.astype(bf16).astype(f32)
    high_tap = (1.0 - low).astype(bf16).astype(f32)
    block = jnp.bitwise_and(lax.shift_right_logical(line, 5), 15) * 16 + lax.shift_right_logical(line, 9)
    place = jnp.bitwise_and(line, BLOCK - 1)
    rows = iota((BLOCK, TABLE), 0)
    nothing = jnp.zeros((BLOCK, TABLE), f32)
    inside = jnp.where(rows == place, low_tap, jnp.where(rows == place + 1, high_tap, nothing))
    beyond = jnp.where(place == BLOCK - 1, high_tap, 0.0)
    chosen = jnp.where(iota((DEVICES, TABLE), 0).astype(jnp.int16) == block.astype(jnp.int16), jnp.ones((), bf16), jnp.zeros((), bf16))
    return chosen, inside, beyond


def score_kernel(got, lower, weight, table_in, part, weighted, misc, table, wide, done):
    fetch = pltpu.make_async_copy(table_in, table, done)
    fetch.start()
    wide[...] = got[...].astype(f32)
    quarter = [wide[pl.ds(a, DEVICES, stride=4), :].astype(bf16) for a in range(4)]
    to, frm = iota((LANE, LANE), 0), iota((LANE, LANE), 1)
    spread = jnp.zeros((LANE, LANE), f32)
    for c, factor in enumerate(FACTOR):
        spread = jnp.where((to % 8 == c) & (frm == to - c + factor), 1.0, spread)
    same = identity()
    both = jnp.concatenate([same, spread.astype(bf16)], axis=0)
    heavy = []
    for n in range(2):
        pair = dot(both, quarter[n], ((1,), (1,)))
        product = pair[:LANE] * pair[LANE:]
        weighted[n * LANE : (n + 1) * LANE, :] = product
        top = product.astype(bf16)
        rest = (product - top.astype(f32)).astype(bf16)
        heavy.append(jnp.concatenate([top, rest, top], axis=0))
    third = dot(same, quarter[2], ((1,), (1,)))
    fourth = dot(same, quarter[3], ((1,), (1,)))
    misc[0:8, :] = fourth[32:40, :]
    misc[8:40, :] = fourth[48:80, :] + fourth[80:112, :]
    lines = jnp.concatenate([third, fourth[:BLOCK]], axis=0)
    first = [lines[c * BLOCK : c * BLOCK + 1] for c in range(5)] + [jnp.zeros((3, DEVICES), f32)]
    near = pltpu.roll(jnp.concatenate(first, axis=0), DEVICES - 16, 1)
    at = iota((8, DEVICES), 1)
    across = jnp.where(at < DEVICES - 1, pltpu.roll(near, DEVICES - 1, 1), pltpu.roll(near, 15, 1))
    following = jnp.where(at < DEVICES - 16, near, across)
    lines = jnp.concatenate([lines, following, jnp.zeros((8, DEVICES), f32)], axis=0).astype(bf16)
    tables = []
    for s in range(ROWS):
        chosen, inside, beyond = taps(lower, weight, s)
        found = dot(lines, chosen, ((1,), (0,)))
        for c in range(5):
            tables.append(
                jnp.sum(found[c * BLOCK : (c + 1) * BLOCK] * inside, axis=0, keepdims=True)
                + found[5 * BLOCK + c : 5 * BLOCK + c + 1] * beyond
            )
        tables.append(jnp.zeros((3, TABLE), f32))
    slices = jnp.concatenate(tables, axis=0).T
    top = slices.astype(bf16)
    rest = (slices - top.astype(f32)).astype(bf16)
    slices = jnp.concatenate([top, top, rest], axis=1)
    number = iota((TABLE, DEVICES), 0).astype(f32)
    sums = []
    for n in range(2):
        products = dot(slices, heavy[n], ((1,), (0,)))
        for o in range(SLOTS):
            asked = misc[n * SLOTS + o : n * SLOTS + o + 1, :]
            sums.append(jnp.sum(jnp.where(number == asked, products, 0.0), axis=0, keepdims=True))
    part[...] = jnp.broadcast_to(jnp.concatenate(sums, axis=0)[None], part.shape)
    fetch.wait()


def relay_kernel(got, out):
    out[...] = jnp.broadcast_to(jnp.sum(got[...], axis=0, keepdims=True), out.shape)


def back_kernel(got, weighted, misc, lower, weight, out, assignment, spreads, blocks, wide, norm_scale):
    scores = jnp.sum(got[...], axis=0) * norm_scale
    raised = jnp.exp(3.0 * jnp.tanh(scores))
    number = iota((TABLE, DEVICES), 0).astype(f32)
    me = lax.axis_index("img") * 16 + lax.axis_index("vol")
    mine = iota((1, DEVICES), 1) == me
    lane4 = iota((1, SLOTS), 1)
    summed = jnp.zeros((LANE, TABLE), f32)
    for n in range(2):
        group = raised[n * SLOTS : (n + 1) * SLOTS]
        share = group / jnp.sum(group, axis=0, keepdims=True)
        own = jnp.zeros((1, SLOTS), f32)
        table = jnp.zeros((TABLE, DEVICES), f32)
        for o in range(SLOTS):
            row = share[o : o + 1]
            asked = misc[n * SLOTS + o : n * SLOTS + o + 1, :]
            table = table + jnp.where(number == asked, row, 0.0)
            one = jnp.sum(jnp.where(mine, row, 0.0), axis=1, keepdims=True)
            own = jnp.where(lane4 == o, one, own)
        assignment[n : n + 1, :] = own
        summed = summed + dot(
            weighted[n * LANE : (n + 1) * LANE, :].astype(bf16), table.astype(bf16), ((1,), (1,))
        )
    for s in range(ROWS):
        chosen, inside, beyond = taps(lower, weight, s)
        rows = summed[s * 8 : (s + 1) * 8]
        at = pl.ds(s * TABLE, TABLE)
        for c in range(8):
            spreads[c * BLOCK : (c + 1) * BLOCK, at] = (rows[c : c + 1] * inside).astype(bf16)
        spreads[8 * BLOCK : 8 * BLOCK + 16, at] = jnp.concatenate(
            [rows * beyond, jnp.zeros((8, TABLE), f32)], axis=0
        ).astype(bf16)
        blocks[:, at] = chosen
    total = dot(spreads[...], blocks[...], ((1,), (1,)))
    last = total[8 * BLOCK : 8 * BLOCK + 8]
    at = iota((8, DEVICES), 1)
    across = jnp.where(at >= 1, pltpu.roll(last, 17, 1), pltpu.roll(last, 1, 1))
    carried = jnp.where(at >= 16, pltpu.roll(last, 16, 1), across)
    first = iota((BLOCK, DEVICES), 0) == 0
    accum = [
        total[c * BLOCK : (c + 1) * BLOCK] + jnp.where(first, carried[c : c + 1], 0.0) for c in range(8)
    ]
    ratio = misc[8:40, :]
    filtered = [accum[c] / (accum[FACTOR[c]] + ratio) for c in range(5)]
    wide[pl.ds(0, DEVICES, stride=2), :] = jnp.concatenate(filtered[:4], axis=0).T
    wide[pl.ds(1, DEVICES, stride=2), :] = jnp.concatenate(
        [filtered[4], jnp.zeros((LANE - BLOCK, DEVICES), f32)], axis=0
    ).T
    out[...] = wide[...].astype(bf16)


def field_kernel(got, table, out, wide):
    wide[...] = got[...].astype(f32)
    early = wide[pl.ds(0, DEVICES, stride=2), :].T
    late = wide[pl.ds(1, DEVICES, stride=2), :].T[:BLOCK]
    block = [early[c * BLOCK : (c + 1) * BLOCK] for c in range(4)]
    real = jnp.concatenate([block[0], block[2], late[:, :LANE]], axis=1)
    imaginary = jnp.concatenate([block[1], block[3], late[:, LANE:]], axis=1)
    both = jnp.concatenate([real, imaginary], axis=0).astype(bf16)
    waves = dot(both, table[...], ((1,), (0,)))
    out[:, :WIDTH] = waves[:BLOCK, :WIDTH] - waves[BLOCK:, WIDTH:]
    out[:, WIDTH:] = waves[:BLOCK, WIDTH:] + waves[BLOCK:, :WIDTH]


def whole():
    return pl.BlockSpec(memory_space=pltpu.VMEM)


def in_hbm(x):
    return pltpu.with_memory_space_constraint(x, pltpu.HBM)


def kernel_call(kernel, outs, scratch, in_specs):
    return pl.pallas_call(
        kernel,
        out_shape=outs,
        in_specs=in_specs,
        out_specs=jax.tree.map(lambda _: whole(), outs),
        scratch_shapes=scratch,
        compiler_params=pltpu.CompilerParams(vmem_limit_bytes=VMEM_LIMIT),
    )


def on_device(orientations, images, ctf_values, volume, line_index, line_weight, noise_ratio):
    norm_scale = 1.0 / math.sqrt(2.0 * ROWS * WIDTH)
    hbm = pl.BlockSpec(memory_space=pltpu.HBM)
    struct = jax.ShapeDtypeStruct
    message, lower, weight = kernel_call(
        pack_kernel,
        (
            struct((4 * DEVICES, LANE), bf16),
            struct((ROWS, TABLE), jnp.int32),
            struct((ROWS, TABLE), f32),
        ),
        [
            pltpu.VMEM((BLOCK, 2 * WIDTH), bf16),
            pltpu.VMEM((BLOCK, WIDTH), bf16),
            pltpu.VMEM((BLOCK, 2 * WIDTH), bf16),
            pltpu.SMEM((SLOTS, BLOCK), jnp.int32),
            pltpu.SMEM((BLOCK,), f32),
            pltpu.VMEM((512, LANE), f32),
            pltpu.VMEM((4 * DEVICES, LANE), f32),
            pltpu.SemaphoreType.DMA((7,)),
        ],
        [hbm] * 7,
    )(
        in_hbm(images.reshape(BLOCK, 2 * WIDTH)),
        in_hbm(ctf_values.reshape(BLOCK, WIDTH)),
        in_hbm(volume),
        in_hbm(orientations.T),
        in_hbm(noise_ratio),
        in_hbm(line_index.T),
        in_hbm(line_weight.T),
    )
    got = lax.all_to_all(message.reshape(DEVICES, 4, LANE), ORDER, 0, 0, tiled=True)
    part, weighted, misc, table = kernel_call(
        score_kernel,
        (
            struct((16, 8, DEVICES), f32),
            struct((DEVICES, DEVICES), f32),
            struct((40, DEVICES), f32),
            struct((WIDTH, 2 * WIDTH), bf16),
        ),
        [pltpu.VMEM((4 * DEVICES, LANE), f32), pltpu.SemaphoreType.DMA],
        [whole()] * 3 + [hbm],
    )(got.reshape(4 * DEVICES, LANE), lower, weight, in_hbm(jnp.asarray(inverse_rows())))
    part = lax.all_to_all(part, OTHER_ORDER, 0, 0, axis_index_groups=FLAT, tiled=True)
    part = kernel_call(relay_kernel, struct((16, 8, DEVICES), f32), [], [whole()])(part)
    part = lax.all_to_all(part, OTHER_ORDER, 0, 0, axis_index_groups=DEEP, tiled=True)
    message, assignment = kernel_call(
        functools.partial(back_kernel, norm_scale=norm_scale),
        (struct((2 * DEVICES, LANE), bf16), struct((2, SLOTS), f32)),
        [
            pltpu.VMEM((8 * BLOCK + 16, ROWS * TABLE), bf16),
            pltpu.VMEM((DEVICES, ROWS * TABLE), bf16),
            pltpu.VMEM((2 * DEVICES, LANE), f32),
        ],
        [whole()] * 5,
    )(part, weighted, misc, lower, weight)
    got = lax.all_to_all(message.reshape(DEVICES, 2, LANE), ORDER, 0, 0, tiled=True)
    density_map = kernel_call(
        field_kernel,
        struct((BLOCK, 2 * WIDTH), f32),
        [pltpu.VMEM((2 * DEVICES, LANE), f32)],
        [whole()] * 2,
    )(got.reshape(2 * DEVICES, LANE), table)
    return (assignment, density_map)


def solution(mesh):
    return jax.shard_map(
        on_device,
        mesh=mesh,
        in_specs=(
            P("img", None),
            P(("img", "vol"), None, None),
            P(("img", "vol"), None, None),
            P("vol", None),
            P(),
            P(),
            P(("vol", "img")),
        ),
        out_specs=(P(("img", "vol"), None), P(("vol", "img"), None)),
        check_vma=False,
    )
```

```python
import functools
import math

import jax
import jax.numpy as jnp
import numpy as np
from jax import lax
from jax.experimental import pallas as pl
from jax.experimental.pallas import tpu as pltpu
from jax.sharding import PartitionSpec as P

WIDTH = 640
ROWS = 16
TABLE = 256
SLOTS = 4
LINES = 8192
BANDS = ((0, 1, 4), (2, 3, 4))
LANE = 128
BLOCK = 32
DEVICES = 256
FACTOR = (5, 5, 6, 6, 7, 5, 6, 7)
ORDER = ("img", "vol")
OTHER_ORDER = ("vol", "img")
FLAT = [[(8 * xh + 2 * y + c) * 16 + 8 * xl + z for xl in range(2) for xh in range(2) for y in range(4)] for z in range(8) for c in range(2)]
DEEP = [[(8 * xh + 2 * y + c) * 16 + 8 * xl + z for z in range(8) for c in range(2)] for xl in range(2) for xh in range(2) for y in range(4)]
VMEM_LIMIT = 48 * 1024 * 1024

f32 = jnp.float32
bf16 = jnp.bfloat16


def columns_of(half):
    first, second, last = BANDS[half]
    re = lambda band: LANE * band
    im = lambda band: WIDTH + LANE * band
    return (re(first), im(first), re(second), im(second), im(last) if half else re(last))


def inverse_rows():
    k = np.arange(WIDTH)
    angle = (np.outer(k, k) % WIDTH) * (2.0 * np.pi / WIDTH)
    table = np.concatenate([np.cos(angle), np.sin(angle)], 1) / np.sqrt(WIDTH)
    bands = (BANDS[0][0], BANDS[1][0], BANDS[0][1], BANDS[1][1], BANDS[0][2])
    rows = np.concatenate([np.arange(LANE * band, LANE * band + LANE) for band in bands])
    return np.asarray(table[rows], dtype=jnp.bfloat16)


def iota(shape, dim):
    return lax.broadcasted_iota(jnp.int32, shape, dim)


def dot(a, b, dims, precision=None):
    return lax.dot_general(a, b, (dims, ((), ())), precision=precision, preferred_element_type=f32)


def identity():
    return jnp.where(iota((LANE, LANE), 0) == iota((LANE, LANE), 1), 1.0, 0.0).astype(bf16)


def pack_kernel(
    images_in, ctf_in, volume_in, orientations_in, noise_in, index_in, weight_in, out, lower, weight,
    images, ctf, volume, orientations, noise, mixed, wide, done,
):
    copies = [
        pltpu.make_async_copy(source, target, done.at[n])
        for n, (source, target) in enumerate(
            (
                (orientations_in, orientations),
                (noise_in, noise),
                (index_in, lower),
                (weight_in, weight),
                (images_in, images),
                (ctf_in, ctf),
                (volume_in.at[pl.ds(pl.multiple_of(lax.axis_index("img") * BLOCK, BLOCK), BLOCK), :], volume),
            )
        )
    ]
    for copy in copies:
        copy.start()
    same = identity()
    for copy in copies:
        copy.wait()
    own = lax.axis_index("vol") * 2
    row8 = iota((16, LANE), 0)
    asked = jnp.zeros((16, LANE), f32)
    for r in range(2 * SLOTS):
        value = orientations[r % SLOTS, own + r // SLOTS].astype(f32)
        asked = jnp.where(row8 == r, value, asked)
    row32 = iota((BLOCK, LANE), 0)
    ratio = jnp.zeros((BLOCK, LANE), f32)
    for r in range(BLOCK):
        ratio = jnp.where(row32 == r, noise[r], ratio)
    ratio_top = ratio.astype(bf16)
    ratio_rest = (ratio - ratio_top.astype(f32)).astype(bf16)
    common = [asked.astype(bf16), ratio_top, ratio_rest, jnp.zeros((16, LANE), bf16)]
    for half in range(2):
        starts = columns_of(half)
        pieces = [images[:, start : start + LANE] for start in starts]
        pieces += [ctf[:, LANE * band : LANE * band + LANE] for band in BANDS[half]]
        for c, piece in enumerate(pieces):
            piece = piece.astype(f32)
            for n in range(2):
                mixed[pl.ds(half * 256 + n * LANE + c, ROWS, stride=8), :] = piece[n * ROWS : (n + 1) * ROWS]
        others = jnp.concatenate([volume[:, start : start + LANE] for start in starts] + common, axis=0)
        left = dot(same, mixed[half * 256 : (half + 1) * 256, :].astype(bf16), ((1,), (1,)))
        right = dot(same, others, ((1,), (1,)))
        base = half * 4 * LANE
        wide[pl.ds(base, LANE, stride=4), :] = left[:, :LANE]
        wide[pl.ds(base + 1, LANE, stride=4), :] = left[:, LANE:]
        wide[pl.ds(base + 2, LANE, stride=4), :] = right[:, :LANE]
        wide[pl.ds(base + 3, LANE, stride=4), :] = right[:, LANE:]
    out[...] = wide[...].astype(bf16)


def taps(lower, weight, s):
    line = lower[s : s + 1, :]
    low = weight[s : s + 1, :]
    low_tap = low.astype(bf16).astype(f32)
    high_tap = (1.0 - low).astype(bf16).astype(f32)
    block = jnp.bitwise_and(lax.shift_right_logical(line, 5), 15) * 16 + lax.shift_right_logical(line, 9)
    place = jnp.bitwise_and(line, BLOCK - 1)
    rows = iota((BLOCK, TABLE), 0)
    nothing = jnp.zeros((BLOCK, TABLE), f32)
    inside = jnp.where(rows == place, low_tap, jnp.where(rows == place + 1, high_tap, nothing))
    beyond = jnp.where(place == BLOCK - 1, high_tap, 0.0)
    chosen = jnp.where(iota((DEVICES, TABLE), 0).astype(jnp.int16) == block.astype(jnp.int16), jnp.ones((), bf16), jnp.zeros((), bf16))
    return chosen, inside, beyond


def score_kernel(got, lower, weight, table_in, part, weighted, misc, table, wide, done):
    fetch = pltpu.make_async_copy(table_in, table, done)
    fetch.start()
    wide[...] = got[...].astype(f32)
    quarter = [wide[pl.ds(a, DEVICES, stride=4), :].astype(bf16) for a in range(4)]
    to, frm = iota((LANE, LANE), 0), iota((LANE, LANE), 1)
    spread = jnp.zeros((LANE, LANE), f32)
    for c, factor in enumerate(FACTOR):
        spread = jnp.where((to % 8 == c) & (frm == to - c + factor), 1.0, spread)
    same = identity()
    both = jnp.concatenate([same, spread.astype(bf16)], axis=0)
    heavy = []
    for n in range(2):
        pair = dot(both, quarter[n], ((1,), (1,)))
        product = pair[:LANE] * pair[LANE:]
        weighted[n * LANE : (n + 1) * LANE, :] = product
        top = product.astype(bf16)
        rest = (product - top.astype(f32)).astype(bf16)
        heavy.append(jnp.concatenate([top, rest, top], axis=0))
    third = dot(same, quarter[2], ((1,), (1,)))
    fourth = dot(same, quarter[3], ((1,), (1,)))
    misc[0:8, :] = fourth[32:40, :]
    misc[8:40, :] = fourth[48:80, :] + fourth[80:112, :]
    lines = jnp.concatenate([third, fourth[:BLOCK]], axis=0)
    first = [lines[c * BLOCK : c * BLOCK + 1] for c in range(5)] + [jnp.zeros((3, DEVICES), f32)]
    near = pltpu.roll(jnp.concatenate(first, axis=0), DEVICES - 16, 1)
    at = iota((8, DEVICES), 1)
    across = jnp.where(at < DEVICES - 1, pltpu.roll(near, DEVICES - 1, 1), pltpu.roll(near, 15, 1))
    following = jnp.where(at < DEVICES - 16, near, across)
    lines = jnp.concatenate([lines, following, jnp.zeros((8, DEVICES), f32)], axis=0).astype(bf16)
    tables = []
    for s in range(ROWS):
        chosen, inside, beyond = taps(lower, weight, s)
        found = dot(lines, chosen, ((1,), (0,)))
        for c in range(5):
            tables.append(
                jnp.sum(found[c * BLOCK : (c + 1) * BLOCK] * inside, axis=0, keepdims=True)
                + found[5 * BLOCK + c : 5 * BLOCK + c + 1] * beyond
            )
        tables.append(jnp.zeros((3, TABLE), f32))
    slices = jnp.concatenate(tables, axis=0).T
    top = slices.astype(bf16)
    rest = (slices - top.astype(f32)).astype(bf16)
    slices = jnp.concatenate([top, top, rest], axis=1)
    number = iota((TABLE, DEVICES), 0).astype(f32)
    sums = []
    for n in range(2):
        products = dot(slices, heavy[n], ((1,), (0,)))
        for o in range(SLOTS):
            asked = misc[n * SLOTS + o : n * SLOTS + o + 1, :]
            sums.append(jnp.sum(jnp.where(number == asked, products, 0.0), axis=0, keepdims=True))
    part[...] = jnp.broadcast_to(jnp.concatenate(sums, axis=0)[None], part.shape)
    fetch.wait()


def relay_kernel(got, out):
    out[...] = jnp.broadcast_to(jnp.sum(got[...], axis=0, keepdims=True), out.shape)


def back_kernel(got, weighted, misc, lower, weight, out, assignment, spreads, blocks, wide, norm_scale):
    scores = jnp.sum(got[...], axis=0) * norm_scale
    raised = jnp.exp(3.0 * jnp.tanh(scores))
    number = iota((TABLE, DEVICES), 0).astype(f32)
    me = lax.axis_index("img") * 16 + lax.axis_index("vol")
    mine = iota((1, DEVICES), 1) == me
    lane4 = iota((1, SLOTS), 1)
    heavy, shares = [], []
    for n in range(2):
        group = raised[n * SLOTS : (n + 1) * SLOTS]
        share = group / jnp.sum(group, axis=0, keepdims=True)
        own = jnp.zeros((1, SLOTS), f32)
        table = jnp.zeros((TABLE, DEVICES), f32)
        for o in range(SLOTS):
            row = share[o : o + 1]
            asked = misc[n * SLOTS + o : n * SLOTS + o + 1, :]
            table = table + jnp.where(number == asked, row, 0.0)
            one = jnp.sum(jnp.where(mine, row, 0.0), axis=1, keepdims=True)
            own = jnp.where(lane4 == o, one, own)
        assignment[n : n + 1, :] = own
        heavy.append(weighted[n * LANE : (n + 1) * LANE, :].astype(bf16))
        shares.append(table.astype(bf16))
    summed = dot(jnp.concatenate(heavy, axis=1), jnp.concatenate(shares, axis=1), ((1,), (1,)))
    for s in range(ROWS):
        chosen, inside, beyond = taps(lower, weight, s)
        rows = summed[s * 8 : (s + 1) * 8]
        at = pl.ds(s * TABLE, TABLE)
        for c in range(8):
            spreads[c * BLOCK : (c + 1) * BLOCK, at] = (rows[c : c + 1] * inside).astype(bf16)
        spreads[8 * BLOCK : 8 * BLOCK + 16, at] = jnp.concatenate(
            [rows * beyond, jnp.zeros((8, TABLE), f32)], axis=0
        ).astype(bf16)
        blocks[:, at] = chosen
    total = dot(spreads[...], blocks[...], ((1,), (1,)))
    last = total[8 * BLOCK : 8 * BLOCK + 8]
    at = iota((8, DEVICES), 1)
    across = jnp.where(at >= 1, pltpu.roll(last, 17, 1), pltpu.roll(last, 1, 1))
    carried = jnp.where(at >= 16, pltpu.roll(last, 16, 1), across)
    first = iota((BLOCK, DEVICES), 0) == 0
    accum = [
        total[c * BLOCK : (c + 1) * BLOCK] + jnp.where(first, carried[c : c + 1], 0.0) for c in range(8)
    ]
    ratio = misc[8:40, :]
    filtered = [accum[c] / (accum[FACTOR[c]] + ratio) for c in range(5)]
    wide[pl.ds(0, DEVICES, stride=2), :] = jnp.concatenate(filtered[:4], axis=0).T
    wide[pl.ds(1, DEVICES, stride=2), :] = jnp.concatenate(
        [filtered[4], jnp.zeros((LANE - BLOCK, DEVICES), f32)], axis=0
    ).T
    out[...] = wide[...].astype(bf16)


def field_kernel(got, table, out, wide):
    wide[...] = got[...].astype(f32)
    early = wide[pl.ds(0, DEVICES, stride=2), :].T
    late = wide[pl.ds(1, DEVICES, stride=2), :].T[:BLOCK]
    block = [early[c * BLOCK : (c + 1) * BLOCK] for c in range(4)]
    real = jnp.concatenate([block[0], block[2], late[:, :LANE]], axis=1)
    imaginary = jnp.concatenate([block[1], block[3], late[:, LANE:]], axis=1)
    both = jnp.concatenate([real, imaginary], axis=0).astype(bf16)
    waves = dot(both, table[...], ((1,), (0,)))
    out[:, :WIDTH] = waves[:BLOCK, :WIDTH] - waves[BLOCK:, WIDTH:]
    out[:, WIDTH:] = waves[:BLOCK, WIDTH:] + waves[BLOCK:, :WIDTH]


def whole():
    return pl.BlockSpec(memory_space=pltpu.VMEM)


def in_hbm(x):
    return pltpu.with_memory_space_constraint(x, pltpu.HBM)


def kernel_call(kernel, outs, scratch, in_specs):
    return pl.pallas_call(
        kernel,
        out_shape=outs,
        in_specs=in_specs,
        out_specs=jax.tree.map(lambda _: whole(), outs),
        scratch_shapes=scratch,
        compiler_params=pltpu.CompilerParams(vmem_limit_bytes=VMEM_LIMIT),
    )


def on_device(orientations, images, ctf_values, volume, line_index, line_weight, noise_ratio):
    norm_scale = 1.0 / math.sqrt(2.0 * ROWS * WIDTH)
    hbm = pl.BlockSpec(memory_space=pltpu.HBM)
    struct = jax.ShapeDtypeStruct
    message, lower, weight = kernel_call(
        pack_kernel,
        (
            struct((4 * DEVICES, LANE), bf16),
            struct((ROWS, TABLE), jnp.int32),
            struct((ROWS, TABLE), f32),
        ),
        [
            pltpu.VMEM((BLOCK, 2 * WIDTH), bf16),
            pltpu.VMEM((BLOCK, WIDTH), bf16),
            pltpu.VMEM((BLOCK, 2 * WIDTH), bf16),
            pltpu.SMEM((SLOTS, BLOCK), jnp.int32),
            pltpu.SMEM((BLOCK,), f32),
            pltpu.VMEM((512, LANE), f32),
            pltpu.VMEM((4 * DEVICES, LANE), f32),
            pltpu.SemaphoreType.DMA((7,)),
        ],
        [hbm] * 7,
    )(
        in_hbm(images.reshape(BLOCK, 2 * WIDTH)),
        in_hbm(ctf_values.reshape(BLOCK, WIDTH)),
        in_hbm(volume),
        in_hbm(orientations.T),
        in_hbm(noise_ratio),
        in_hbm(line_index.T),
        in_hbm(line_weight.T),
    )
    got = lax.all_to_all(message.reshape(DEVICES, 4, LANE), ORDER, 0, 0, tiled=True)
    part, weighted, misc, table = kernel_call(
        score_kernel,
        (
            struct((16, 8, DEVICES), f32),
            struct((DEVICES, DEVICES), f32),
            struct((40, DEVICES), f32),
            struct((WIDTH, 2 * WIDTH), bf16),
        ),
        [pltpu.VMEM((4 * DEVICES, LANE), f32), pltpu.SemaphoreType.DMA],
        [whole()] * 3 + [hbm],
    )(got.reshape(4 * DEVICES, LANE), lower, weight, in_hbm(jnp.asarray(inverse_rows())))
    part = lax.all_to_all(part, OTHER_ORDER, 0, 0, axis_index_groups=FLAT, tiled=True)
    part = kernel_call(relay_kernel, struct((16, 8, DEVICES), f32), [], [whole()])(part)
    part = lax.all_to_all(part, OTHER_ORDER, 0, 0, axis_index_groups=DEEP, tiled=True)
    message, assignment = kernel_call(
        functools.partial(back_kernel, norm_scale=norm_scale),
        (struct((2 * DEVICES, LANE), bf16), struct((2, SLOTS), f32)),
        [
            pltpu.VMEM((8 * BLOCK + 16, ROWS * TABLE), bf16),
            pltpu.VMEM((DEVICES, ROWS * TABLE), bf16),
            pltpu.VMEM((2 * DEVICES, LANE), f32),
        ],
        [whole()] * 5,
    )(part, weighted, misc, lower, weight)
    got = lax.all_to_all(message.reshape(DEVICES, 2, LANE), ORDER, 0, 0, tiled=True)
    density_map = kernel_call(
        field_kernel,
        struct((BLOCK, 2 * WIDTH), f32),
        [pltpu.VMEM((2 * DEVICES, LANE), f32)],
        [whole()] * 2,
    )(got.reshape(2 * DEVICES, LANE), table)
    return (assignment, density_map)


def solution(mesh):
    return jax.shard_map(
        on_device,
        mesh=mesh,
        in_specs=(
            P("img", None),
            P(("img", "vol"), None, None),
            P(("img", "vol"), None, None),
            P("vol", None),
            P(),
            P(),
            P(("vol", "img")),
        ),
        out_specs=(P(("img", "vol"), None), P(("vol", "img"), None)),
        check_vma=False,
    )
```
